32 devices in a mesh: runs: 2 (over y), gx: 4 (over z), gy: 4 (over x, core).
Axes of the slice: x: 2, y: 2, z: 4, core: 2. Of those that a mesh axis runs over, the one named last changes fastest.
Arguments:
- offsets: float32 [1024, 3, 128], P(('runs', 'gx', 'gy')), parts along dimension 0, may hold values from 0.5 to 1.5
- cell_index: int32 [1024, 128], P(('runs', 'gx', 'gy')), parts along dimension 0, may hold values from 0 to 23
- velocity: float32 [1024, 3, 128], P(('runs', 'gx', 'gy')), parts along dimension 0, may hold values from -6 to 6
- affine: float32 [1024, 9, 128], P(('runs', 'gx', 'gy')), parts along dimension 0, may hold values from -3 to 3
- strain: float32 [1024, 9, 128], P(('runs', 'gx', 'gy')), parts along dimension 0, may hold values from -0.1 to 0.1
- particle_mass: float32 [1024, 128], P(('runs', 'gx', 'gy')), parts along dimension 0, may hold values from 0.5 to 2
- owner_row: int32 [1024, 1], P(('runs', 'gx', 'gy')), parts along dimension 0, may hold values from 0 to 3; in each aligned block of 32 rows (0 to 31, 32 to 63, ...) at most 24 rows name the same one
- anchor_xy: int32 [1024, 2], P(('runs', 'gx', 'gy')), parts along dimension 0, may hold values from -2 to 14
- anchor_z: int32 [1024], P(('runs', 'gx', 'gy')), parts along dimension 0, may hold values from 0 to 120
Outputs:
- final_velocity: float32 [1024, 3, 128], P(('runs', 'gx', 'gy')), parts along dimension 0
- final_affine: float32 [1024, 9, 128], P(('runs', 'gx', 'gy')), parts along dimension 0
- final_deform: float32 [1024, 9, 128], P(('runs', 'gx', 'gy')), parts along dimension 0
The draws below stay inside these ranges and needn't reach their ends.
There are 2 independent parts, one for each index of `runs`. The reference program is written for one: setup_inputs(seed, part) draws one part's arguments, and reference() takes and returns one part's arrays. A program takes and returns all parts, laid end to end along the dimension named above; each array names one. Nothing has to cross between parts.
Inputs may be any that keep to these rules, and one draw needn't show every extreme that they name: `owner_row`: among the 32 bins of one device, in aligned blocks of 32 bins, at most 24 name the same row.
All inputs are finite; a program needn't handle non-finite values.
Results may differ from the reference program's by a relative error of at most 0.0003.
Values sent between devices are 32-bit elements; how exact they have to be, the bound alone decides.
No kernel may reach another device: no remote copies, remote signals or barrier semaphores. Data moves between devices by JAX's collectives and lax.ppermute only.
A program may use at most 128 MiB of HBM per device.

```python
import math
import jax
import jax.numpy as jnp
import numpy as np
from jax import lax

TILE = 16
CZ = 128
BINS_DEV = 32
BIN = 128
SUBSTEPS = 4
NBINS = 512
MOST = 24
N_GX = 4
N_GY = 4


def plant(result, stream_key, least, high):
    dims = result.shape
    place = [jax.random.randint(jax.random.fold_in(stream_key, axis), (), 0, dims[axis]) for axis in range(len(dims))]
    result = result.at[tuple(place)].set(least)
    longest = dims.index(max(dims))
    place[longest] = (place[longest] + 1) % dims[longest]
    return result.at[tuple(place)].set(high)


def shard_levels(key, shape, split, least, largest):
    def one(dim, blocks):
        steps = jax.random.uniform(jax.random.fold_in(jax.random.fold_in(key, 6), dim), (blocks,), jnp.float32, least / len(split), largest / len(split))
        return jnp.repeat(jnp.exp(steps), shape[dim] // blocks).reshape((-1,) + (1,) * (len(shape) - dim - 1))

    factor_of = one(*split[0])
    for cut in split[1:]:
        factor_of = factor_of * one(*cut)
    return factor_of


def shared_out(stream_key, own, number, rows, count, top, bound, skew):
    sequence = jax.random.permutation(stream_key, count)
    packed, usual = load_shares(count, rows * top, bound, skew, True), load_shares(count, rows * top, bound, skew, False)
    places = jnp.arange(count)

    def named(lengths, turn):
        used = int((lengths > 0).sum())
        fixed = max(1, used // 4)
        passed = fixed + (places - fixed + turn * (used - fixed)) % max(1, count - fixed)
        return jnp.zeros((count,), jnp.int32).at[sequence[jnp.where(places < fixed, places, passed)]].set(jnp.asarray(lengths, jnp.int32))

    lengths = jnp.where(number % 4 == 0, named(packed, number // 4), named(usual, number - number // 4 - 1))
    mixed = jax.random.permutation(jax.random.fold_in(own, 3), count)
    source_of, taker = mixed[0:count // 2 * 2:2], mixed[1:count // 2 * 2:2]
    margin = jnp.minimum(lengths[source_of] - 1, bound - lengths[taker]) // 2
    margin = jnp.where((source_of == sequence[0]) | (taker == sequence[0]) | (lengths[taker] == 0), 0, jnp.maximum(margin, 0))
    passed = jax.random.randint(jax.random.fold_in(own, 4), (count // 2,), 0, 1 << 20) % (margin + 1)
    lengths = lengths.at[source_of].add(-passed).at[taker].add(passed)
    members = jnp.searchsorted(jnp.cumsum(lengths), jnp.arange(rows * top), side="right").astype(jnp.int32)
    table = members.reshape(top, rows).T
    table = table[jax.random.permutation(jax.random.fold_in(own, 1), rows)]
    turn = jax.random.randint(jax.random.fold_in(own, 2), (rows, 1), 0, top)
    return jnp.take_along_axis(table, (jnp.arange(top)[None, :] + turn) % top, axis=1)


def load_shares(amount, total, limit, lean, full):
    weights = [(1 << 20) // math.isqrt(grade ** lean) + 1 for grade in range(1, amount + 1)]
    largest = limit if full else min(limit, max(-(-total // amount), total * weights[0] // sum(weights)))
    least = 1 if total - largest >= amount - 1 else 0
    counts, rest = [largest] + [least] * (amount - 1), total - largest - least * (amount - 1)
    while rest > 0:
        free = [i for i in range(1, amount) if counts[i] < largest] or [i for i in range(1, amount) if counts[i] < limit]
        mass, left = sum([weights[i] for i in free]), rest
        for i in free:
            addition = min(limit - counts[i], max(1, left * weights[i] // mass), rest)
            counts[i] = counts[i] + addition
            rest = rest - addition
    return np.array(counts)


def centred(own_key, shape, width, bound, cuts=(), kind=jnp.bfloat16):
    drawn = width * jax.random.normal(own_key, shape, jnp.float32)
    if cuts:
        drawn = drawn * shard_levels(own_key, shape, cuts, -0.22, 0.18)
    return jnp.clip(drawn, -bound, bound).astype(kind)


def setup_inputs(seed: int = 0, part: int = 0) -> dict:
    splits = jax.random.split(jax.random.key(seed), 10)
    part_keys = jax.random.split(jax.random.fold_in(splits[9], part), 10)
    offsets = jnp.clip(0.5 + 1.0 * jax.random.uniform(part_keys[0], (NBINS, 3, BIN), jnp.float32) ** shard_levels(part_keys[0], (NBINS, 3, BIN), ((0, 16),), -0.2, 0.2), 0.5, 1.5)
    cell_index = plant(jax.random.randint(part_keys[1], (NBINS, BIN), 0, 24), jax.random.fold_in(part_keys[1], 1), 0, 23).astype(jnp.int32)
    velocity = centred(part_keys[2], (NBINS, 3, BIN), 1.0, 6.0, ((0, 16),), jnp.float32)
    affine = centred(part_keys[3], (NBINS, 9, BIN), 0.5, 3.0, ((0, 16),), jnp.float32)
    strain = jnp.clip(jax.random.uniform(part_keys[4], (NBINS, 9, BIN), jnp.float32, -0.1, 0.1) * shard_levels(part_keys[4], (NBINS, 9, BIN), ((0, 16),), -0.4, 0.0), -0.1, 0.1)
    particle_mass = jnp.clip(jnp.exp(math.log(2.0) - 1.3862944 * jax.random.uniform(part_keys[5], (NBINS, BIN), jnp.float32) ** shard_levels(part_keys[5], (NBINS, BIN), ((0, 16),), -0.2, 0.2)), 0.5, 2.0)
    owner_row_keys = jax.random.split(jax.random.fold_in(part_keys[6], 1), NBINS // BINS_DEV)
    owner_row_turns = jax.random.permutation(jax.random.fold_in(part_keys[6], 3), NBINS // BINS_DEV)
    owner_row = jax.vmap(lambda own, number: shared_out(jax.random.fold_in(part_keys[6], 2), own, number, BINS_DEV, N_GX, 1, MOST, 2))(owner_row_keys, owner_row_turns).reshape((NBINS, 1))
    anchor_xy = plant(jax.random.randint(part_keys[7], (NBINS, 2), -2, TILE - 1), jax.random.fold_in(part_keys[7], 1), -2, (TILE - 1) - 1).astype(jnp.int32)
    anchor_z = plant(jax.random.randint(part_keys[8], (NBINS,), 0, CZ - 7), jax.random.fold_in(part_keys[8], 1), 0, (CZ - 7) - 1).astype(jnp.int32)
    return dict(offsets=offsets, cell_index=cell_index, velocity=velocity, affine=affine, strain=strain, particle_mass=particle_mass, owner_row=owner_row, anchor_xy=anchor_xy, anchor_z=anchor_z)


time_step = 0.05
shear_coef = 2.0
bulk_coef = 2.0
gravity = 2.0
mass_floor = 0.25
highest_index = lax.Precision.HIGHEST


def node_grid():
    serial = jnp.arange(128, dtype=jnp.int32)
    return jnp.stack([serial // 32, (serial // 8) % 4, serial % 8])


def axis_weights(fraction, base_cell, extent):
    offsets_of = jnp.arange(extent, dtype=jnp.int32)[None, None, :] - base_cell[:, :, None]
    lower = 0.5 * (1.5 - fraction) ** 2
    middle = 0.75 - (fraction - 1.0) ** 2
    upper = 0.5 * (fraction - 0.5) ** 2
    return (jnp.where(offsets_of == 0, lower[:, :, None], 0.0)
            + jnp.where(offsets_of == 1, middle[:, :, None], 0.0)
            + jnp.where(offsets_of == 2, upper[:, :, None], 0.0))


def stencil(offsets, cell_index):
    base_cell = jnp.stack([cell_index // 12, (cell_index // 6) % 2, cell_index % 6], axis=1)
    weight_x = axis_weights(offsets[:, 0], base_cell[:, 0], 4)
    weight_y = axis_weights(offsets[:, 1], base_cell[:, 1], 4)
    weight_z = axis_weights(offsets[:, 2], base_cell[:, 2], 8)
    kernel_weight = weight_x[:, :, :, None, None] * weight_y[:, :, None, :, None] * weight_z[:, :, None, None, :]
    kernel_weight = kernel_weight.reshape(offsets.shape[0], 128, 128)
    position = base_cell.astype(jnp.float32) + offsets
    return kernel_weight, position


def kirchhoff(deform):
    entries = [[deform[:, 3 * dim_out + dim_in] for dim_in in range(3)] for dim_out in range(3)]
    volume = (entries[0][0] * (entries[1][1] * entries[2][2] - entries[1][2] * entries[2][1])
              - entries[0][1] * (entries[1][0] * entries[2][2] - entries[1][2] * entries[2][0])
              + entries[0][2] * (entries[1][0] * entries[2][1] - entries[1][1] * entries[2][0]))
    log_volume = jnp.log(volume)
    stress = []
    for dim_out in range(3):
        for dim_in in range(3):
            product = entries[dim_out][0] * entries[dim_in][0] + entries[dim_out][1] * entries[dim_in][1] + entries[dim_out][2] * entries[dim_in][2]
            diagonal = 1.0 if dim_out == dim_in else 0.0
            stress.append(shear_coef * (product - diagonal) + bulk_coef * log_volume * diagonal)
    return stress


def deposit(kernel_weight, position, velocity, affine, deform, particle_mass):
    stress = kirchhoff(deform)
    blend = [particle_mass * affine[:, entry_at] - stress[entry_at] for entry_at in range(9)]
    pushed = [sum(blend[3 * dim_out + dim_in] * position[:, dim_in] for dim_in in range(3)) for dim_out in range(3)]
    columns = [particle_mass] + [particle_mass * velocity[:, dim_out] - pushed[dim_out] for dim_out in range(3)] + blend
    source_rank = jnp.stack(columns, axis=1)
    moment_sums = jnp.einsum("axf,afg->xag", source_rank, kernel_weight, precision=highest_index)
    coords = node_grid().astype(jnp.float32)
    momentum = [moment_sums[1 + dim_out] + sum(moment_sums[4 + 3 * dim_out + dim_in] * coords[dim_in] for dim_in in range(3)) for dim_out in range(3)]
    return jnp.stack([moment_sums[0]] + momentum, axis=0)


def collect(kernel_weight, position, offsets, deform, node_velocity):
    coords = node_grid().astype(jnp.float32)
    field_channels = [node_velocity[dim_out] for dim_out in range(3)] + [node_velocity[dim_out] * coords[dim_in] for dim_out in range(3) for dim_in in range(3)]
    gathered_rows = jnp.einsum("ejf,jvf->ejv", jnp.stack(field_channels, axis=0), kernel_weight, precision=highest_index)
    velocity = [gathered_rows[dim_out] for dim_out in range(3)]
    affine = [4.0 * (gathered_rows[3 + 3 * dim_out + dim_in] - velocity[dim_out] * position[:, dim_in]) for dim_out in range(3) for dim_in in range(3)]
    deform_next = [deform[:, 3 * dim_out + dim_in] + time_step * sum(affine[3 * dim_out + dim_mid] * deform[:, 3 * dim_mid + dim_in] for dim_mid in range(3)) for dim_out in range(3) for dim_in in range(3)]
    offsets_next = offsets + time_step * jnp.stack(velocity, axis=1)
    return jnp.stack(velocity, axis=1), jnp.stack(affine, axis=1), jnp.stack(deform_next, axis=1), offsets_next


def grid_velocity(node_sums, start_x, start_y, total_x, total_y):
    grid_shape = node_sums.shape[1:]
    coord_x = start_x + lax.broadcasted_iota(jnp.int32, grid_shape, 0)
    coord_y = start_y + lax.broadcasted_iota(jnp.int32, grid_shape, 1)
    coord_z = lax.broadcasted_iota(jnp.int32, grid_shape, 2)
    divisor = jnp.maximum(node_sums[0], mass_floor)
    inside_x = (coord_x >= 2) & (coord_x < total_x - 2)
    inside_y = (coord_y >= 2) & (coord_y < total_y - 2)
    inside_z = (coord_z >= 2) & (coord_z < grid_shape[2] - 2)
    velocity_x = jnp.where(inside_x, node_sums[1] / divisor, 0.0)
    velocity_y = jnp.where(inside_y, node_sums[2] / divisor, 0.0)
    velocity_z = jnp.where(inside_z, node_sums[3] / divisor - time_step * gravity, 0.0)
    return jnp.stack([velocity_x, velocity_y, velocity_z], axis=0)


def reference(offsets, cell_index, velocity, affine, strain, particle_mass, owner_row, anchor_xy, anchor_z):
    total_x = TILE * N_GX
    total_y = TILE * N_GY
    blocks = NBINS // BINS_DEV
    serial = jnp.arange(NBINS, dtype=jnp.int32)
    column = (serial // BINS_DEV) % N_GY
    corner_x = owner_row[:, 0] * TILE + anchor_xy[:, 0] + 2
    corner_y = column * TILE + anchor_xy[:, 1] + 2
    nodes = node_grid()
    flat_index = ((corner_x[:, None] + nodes[0][None, :]) * (total_y + 4) + corner_y[:, None] + nodes[1][None, :]) * CZ + anchor_z[:, None] + nodes[2][None, :]
    deform = strain + jnp.eye(3, dtype=jnp.float32).reshape(1, 9, 1)

    def split_bins(array):
        return array.reshape((blocks, BINS_DEV) + array.shape[1:])

    def join_bins(array):
        return array.reshape((NBINS,) + array.shape[2:])

    def bin_patches(bin_block):
        kernel_weight, position = stencil(bin_block[0], bin_block[1])
        return deposit(kernel_weight, position, bin_block[2], bin_block[3], bin_block[4], bin_block[5])

    def bin_update(bin_block):
        kernel_weight, position = stencil(bin_block[0], bin_block[1])
        return collect(kernel_weight, position, bin_block[0], bin_block[2], bin_block[3])

    for substep in range(SUBSTEPS):
        patches = lax.map(bin_patches, tuple(split_bins(member) for member in (offsets, cell_index, velocity, affine, deform, particle_mass)))
        patches = jnp.moveaxis(patches, 0, 1).reshape(4, NBINS, 128)
        node_sums = jnp.zeros((4, (total_x + 4) * (total_y + 4) * CZ), jnp.float32).at[:, flat_index].add(patches)
        node_sums = node_sums.reshape(4, total_x + 4, total_y + 4, CZ)[:, 2:total_x + 2, 2:total_y + 2]
        node_velocity = grid_velocity(node_sums, 0, 0, total_x, total_y)
        padded = jnp.pad(node_velocity, ((0, 0), (2, 2), (2, 2), (0, 0)))
        velocity_patch = padded.reshape(3, -1)[:, flat_index]
        velocity_patch = jnp.moveaxis(velocity_patch.reshape(3, blocks, BINS_DEV, 128), 1, 0)
        updated = lax.map(bin_update, (split_bins(offsets), split_bins(cell_index), split_bins(deform), velocity_patch))
        velocity, affine, deform, offsets = tuple(join_bins(member) for member in updated)
    return velocity, affine, deform
```

```python
import functools

import jax
import jax.numpy as jnp
from jax import lax
from jax.experimental import pallas as pl
from jax.experimental.pallas import tpu as pltpu
from jax.sharding import PartitionSpec as P

TILE = 16
CZ = 128
SUBSTEPS = 4
SPAN_Y = 26
LOW_Y = 5
ROWS_X = 4 * SPAN_Y

time_step = 0.05
shear_coef = 2.0
bulk_coef = 2.0
gravity = 2.0
mass_floor = 0.25

F32 = jnp.float32
BF16 = jnp.bfloat16


def split(value):
    high = value.astype(BF16)
    low = (value - high.astype(F32)).astype(BF16)
    return high, low


def quadratic(f):
    lower = 0.5 * (1.5 - f) ** 2
    middle = 0.75 - (f - 1.0) ** 2
    upper = 0.5 * (f - 0.5) ** 2
    return lower, middle, upper


def row_of(ref, at):
    return jnp.broadcast_to(ref[pl.ds(at, 1), :], (8, 128))


def stencil_rows(group, fractions, bases, params):
    def put(row, value):
        params[pl.ds(group * 128 + row, 8, stride=16), :] = value

    for axis in range(2):
        lower, middle, upper = quadratic(fractions[axis])
        first = bases[axis] < 0.5
        put(4 * axis, jnp.where(first, lower, 0.0))
        put(4 * axis + 1, jnp.where(first, middle, lower))
        put(4 * axis + 2, jnp.where(first, upper, middle))
        put(4 * axis + 3, jnp.where(first, 0.0, upper))
        put(8 + axis, bases[axis] + fractions[axis])
    put(10, fractions[2])
    put(11, bases[2])
    for at, value in enumerate(quadratic(fractions[2])):
        put(12 + at, value)


def depth_weights(bins, params, depth):
    serial = lax.broadcasted_iota(jnp.int32, (8, 128), 0).astype(F32)

    def one(at):
        base = at * 16
        t = serial - row_of(params, base + 11)
        w = jnp.where(
            t == 0.0,
            row_of(params, base + 12),
            jnp.where(
                t == 1.0,
                row_of(params, base + 13),
                jnp.where(t == 2.0, row_of(params, base + 14), 0.0),
            ),
        )
        return jnp.concatenate([w, (t - row_of(params, base + 10)) * w], axis=1)

    def pair(at, _):
        value = jnp.concatenate([one(2 * at), one(2 * at + 1)], axis=0)
        high, low = split(value)
        group = at // 8
        row = pl.multiple_of((at % 8) * 16, 16)
        depth[group, pl.ds(row, 16), :] = high
        depth[group, pl.ds(row + 128, 16), :] = high
        depth[group, pl.ds(row + 256, 16), :] = low
        return _

    lax.fori_loop(0, bins // 2, pair, 0, unroll=4)


def y_patterns(params, base, sub):
    upper_half = sub >= 4
    x1 = row_of(params, base + 9)
    weights = []
    moments = []
    for half in range(2):
        w = jnp.where(
            upper_half, row_of(params, base + 5 + 2 * half), row_of(params, base + 4 + 2 * half)
        )
        j = jnp.where(upper_half, 1.0 + 2 * half, 0.0 + 2 * half)
        weights.append(w)
        moments.append(w * (j - x1))
    return weights, moments


def deposit_rows(group, velocity, affine, deform, mass, blends):
    entries = [[deform[3 * a + b] for b in range(3)] for a in range(3)]
    volume = (
        entries[0][0] * (entries[1][1] * entries[2][2] - entries[1][2] * entries[2][1])
        - entries[0][1] * (entries[1][0] * entries[2][2] - entries[1][2] * entries[2][0])
        + entries[0][2] * (entries[1][0] * entries[2][1] - entries[1][1] * entries[2][0])
    )
    log_volume = jnp.log(volume)

    def put(kind, channel, value):
        for half in range(2):
            blends[pl.ds(group * 256 + kind * 8 + half * 4 + channel, 8, stride=32), :] = value

    zero = jnp.zeros_like(mass)
    put(0, 0, mass)
    for b in range(3):
        put(1 + b, 0, zero)
    for a in range(3):
        put(0, 1 + a, mass * velocity[a])
        for b in range(3):
            product = sum(entries[a][c] * entries[b][c] for c in range(3))
            diagonal = 1.0 if a == b else 0.0
            stress = shear_coef * (product - diagonal) + bulk_coef * log_volume * diagonal
            put(1 + b, 1 + a, mass * affine[3 * a + b] - stress)


def scatter_bins(tabs, own_count, lane, sets, sums):
    at_base = own_count
    total = tabs.shape[0] // 2
    for column, patch_ref in enumerate(sets):
        devices = patch_ref.shape[0]
        groups = own_count // 16

        def block(at, _, patch_ref=patch_ref, at_base=at_base, column=column):
            dev = at // groups
            start = pl.multiple_of((at % groups) * 64, 64)
            first = at_base + at * 16
            for slot in range(16):
                row = tabs[first + slot]
                z = tabs[total + first + slot]

                def add(row=row, z=z, slot=slot):
                    patch = patch_ref[dev, pl.ds(start, 64), :]
                    moved = pltpu.roll(patch, (z + (128 - 8 * slot)) & 127, 1)
                    inside = (lane >= z) & (lane < z + 8)
                    moved = jnp.where(inside, moved, 0.0)
                    for i in range(4):
                        place = pl.ds(row + i * ROWS_X, 16)
                        sums[place, :] = sums[place, :] + moved[16 * i : 16 * i + 16]

                if column == 0:
                    add()
                else:
                    pl.when(row >= 0)(add)
            return _

        lax.fori_loop(0, devices * groups, block, 0)
        at_base = at_base + devices * own_count


def fill(blocks):
    return jnp.concatenate(blocks, axis=0)


def kernel(first, last, total_count, *refs):
    refs = list(refs)
    take = lambda n: [refs.pop(0) for _ in range(n)]
    if first:
        offsets_in, cell, velocity_in, affine_in, strain, mass_in = take(6)
        bins = mass_in.shape[0]
    else:
        tabs, patch_own, patch_a, patch_b, inside_ref, state_in = take(6)
        bins = state_in.shape[1]
    if last:
        velocity_out, affine_out, deform_out = take(3)
    else:
        patch_out, state_out = take(2)
    params, depth, wide, wide_low, products = take(5)
    if not first:
        sums, results = take(2)
    if not last:
        blends, products_low = take(2)
    groups = bins // 16
    sub = lax.broadcasted_iota(jnp.int32, (8, 128), 0)
    lane = lax.broadcasted_iota(jnp.int32, (64, 128), 1)
    lane_row = lax.broadcasted_iota(jnp.int32, (1, 128), 1)

    def load8(g8):
        span = pl.ds(g8 * 8, 8)
        if first:
            fractions = [offsets_in[a, span, :] for a in range(3)]
            c = cell[span, :]
            bx = (c >= 12).astype(jnp.int32)
            c = c - 12 * bx
            by = (c >= 6).astype(jnp.int32)
            bases = [bx.astype(F32), by.astype(F32), (c - 6 * by).astype(F32)]
            deform = [
                strain[e, span, :] + (1.0 if e % 4 == 0 else 0.0) for e in range(9)
            ]
            return fractions, bases, deform, mass_in[span, :]
        fractions = [state_in[a, span, :] for a in range(3)]
        bases = [state_in[3 + a, span, :] for a in range(3)]
        deform = [state_in[7 + e, span, :] for e in range(9)]
        return fractions, bases, deform, state_in[6, span, :]

    def store8(g8, fractions, bases, deform, mass):
        span = pl.ds(g8 * 8, 8)
        for a in range(3):
            state_out[a, span, :] = fractions[a]
            state_out[3 + a, span, :] = bases[a]
        state_out[6, span, :] = mass
        for e in range(9):
            state_out[7 + e, span, :] = deform[e]

    if first:
        for g8 in range(bins // 8):
            span = pl.ds(g8 * 8, 8)
            fractions, bases, deform, mass = load8(g8)
            store8(g8, fractions, bases, deform, mass)
            stencil_rows(g8, fractions, bases, params)
            velocity = [velocity_in[a, span, :] for a in range(3)]
            affine = [affine_in[e, span, :] for e in range(9)]
            deposit_rows(g8, velocity, affine, deform, mass, blends)
    else:
        total = tabs.shape[0] // 2
        for g8 in range(bins // 8):
            fractions, bases, _, _ = load8(g8)
            stencil_rows(g8, fractions, bases, params)
        depth_weights(bins, params, depth)

        def clear(at, _):
            for i in range(4):
                sums[pl.ds(tabs[at] + i * ROWS_X, 16), :] = jnp.zeros((16, 128), F32)
            return _

        lax.fori_loop(0, bins, clear, 0, unroll=4)
        scatter_bins(tabs, bins, lane, [patch_own, patch_a, patch_b], sums)
        for g in range(groups):
            compact = jnp.zeros((64, 128), F32)
            for slot in range(16):
                row = tabs[g * 16 + slot]
                z = tabs[total + g * 16 + slot]
                node = fill([sums[pl.ds(row + i * ROWS_X, 16), :] for i in range(4)])
                moved = pltpu.roll(node, (8 * slot + 128 - z) & 127, 1)
                compact = jnp.where(lane // 8 == slot, moved, compact)
            channel = lax.broadcasted_iota(jnp.int32, (64, 128), 0) & 3
            mass = jnp.where(channel == 0, compact, 0.0)
            mass = mass + pltpu.roll(mass, 1, 0)
            mass = mass + pltpu.roll(mass, 2, 0)
            node = compact / jnp.maximum(mass, mass_floor)
            node = node - jnp.where(channel == 3, time_step * gravity, 0.0)
            node = jnp.where(inside_ref[g] > 0.5, node, 0.0)
            high, low = split(node)
            both = jnp.concatenate([high, low], axis=1)
            for slot in range(16):
                keep = (lane_row // 8 == slot).astype(BF16)
                keep = jnp.concatenate([keep, keep], axis=1)
                wide[64 * slot : 64 * slot + 64, :] = both * keep
            products[...] = jnp.dot(
                wide[...], depth[g, 0:256, :], preferred_element_type=F32
            ) + jnp.dot(wide[:, 0:128], depth[g, 256:384, :], preferred_element_type=F32)

            def finish(slot, _, g=g):
                base = (g * 16 + slot) * 16
                weights, moments = y_patterns(params, base, sub)
                x0 = row_of(params, base + 8)
                at = pl.multiple_of(slot * 64, 64)
                plain = [None, None]
                along = [None, None]
                deep = [None, None]
                for i in range(4):
                    wx = row_of(params, base + i)
                    wxi = wx * (i - x0)
                    for half in range(2):
                        place = pl.ds(at + 16 * i + 8 * half, 8)
                        one = products[place, 0:128]
                        two = products[place, 128:256]
                        terms = (wx * one, wxi * one, wx * two)
                        for kept, term in zip((plain, along, deep), terms):
                            kept[half] = term if i == 0 else kept[half] + term
                found = (
                    weights[0] * plain[0] + weights[1] * plain[1],
                    weights[0] * along[0] + weights[1] * along[1],
                    moments[0] * plain[0] + moments[1] * plain[1],
                    weights[0] * deep[0] + weights[1] * deep[1],
                )
                place = pl.multiple_of((g * 16 + slot) * 32, 32)
                for kind, value in enumerate(found):
                    results[pl.ds(place + 8 * kind, 8), :] = value + pltpu.roll(value, 4, 0)
                return _

            lax.fori_loop(0, 16, finish, 0, unroll=4)

        for g8 in range(bins // 8):
            span = pl.ds(g8 * 8, 8)
            fractions, bases, deform, mass = load8(g8)

            def get(kind, a, g8=g8):
                return results[pl.ds(g8 * 256 + kind * 8 + 1 + a, 8, stride=32), :]

            velocity = [get(0, a) for a in range(3)]
            affine = [4.0 * get(1 + b, a) for a in range(3) for b in range(3)]
            deform = [
                deform[3 * a + b]
                + time_step * sum(affine[3 * a + c] * deform[3 * c + b] for c in range(3))
                for a in range(3)
                for b in range(3)
            ]
            if last:
                for a in range(3):
                    velocity_out[a, span, :] = velocity[a]
                for e in range(9):
                    affine_out[e, span, :] = affine[e]
                    deform_out[e, span, :] = deform[e]
            else:
                fractions = [fractions[a] + time_step * velocity[a] for a in range(3)]
                store8(g8, fractions, bases, deform, mass)
                stencil_rows(g8, fractions, bases, params)
                deposit_rows(g8, velocity, affine, deform, mass, blends)

    if not last:
        depth_weights(bins, params, depth)
        for g in range(groups):

            def build(slot, _, g=g):
                base = (g * 16 + slot) * 16
                place = pl.multiple_of((g * 16 + slot) * 32, 32)
                weights, moments = y_patterns(params, base, sub)
                x0 = row_of(params, base + 8)
                pushed, b0, b1, b2 = [blends[pl.ds(place + 8 * k, 8), :] for k in range(4)]
                plain = []
                deep = []
                for i in range(4):
                    wx = row_of(params, base + i)
                    along = (pushed + b0 * (i - x0)) * wx
                    across = b1 * wx
                    depthwise = b2 * wx
                    for half in range(2):
                        plain.append(along * weights[half] + across * moments[half])
                        deep.append(depthwise * weights[half])
                value = jnp.concatenate([fill(plain), fill(deep)], axis=1)
                high, low = split(value)
                at = pl.ds(pl.multiple_of(slot * 64, 64), 64)
                wide[at, :] = high
                wide_low[at, :] = low
                return _

            lax.fori_loop(0, 16, build, 0, unroll=2)
            turned = (((1,), (1,)), ((), ()))
            products[...] = lax.dot_general(
                wide[...], depth[g, 128:384, :], turned, preferred_element_type=F32
            )
            products_low[...] = lax.dot_general(
                wide_low[...], depth[g, 128:256, :], turned, preferred_element_type=F32
            )
            compact = jnp.zeros((64, 128), F32)
            for slot in range(16):
                at = slice(64 * slot, 64 * slot + 64)
                value = products[at, 0:128] + products[at, 128:256] + products_low[at, :]
                compact = jnp.where(lane // 8 == slot, value, compact)
            patch_out[64 * g : 64 * g + 64, :] = compact


def run_kernel(first, last, total_x, bins, operands):
    vmem = pl.BlockSpec(memory_space=pltpu.VMEM)
    smem = pl.BlockSpec(memory_space=pltpu.SMEM)
    shape = lambda *dims: jax.ShapeDtypeStruct(dims, F32)
    if last:
        outs = [shape(3, bins, 128), shape(9, bins, 128), shape(9, bins, 128)]
    else:
        outs = [shape(4 * bins, 128), shape(16, bins, 128)]
    groups = bins // 16
    scratch = [
        pltpu.VMEM((16 * bins, 128), F32),
        pltpu.VMEM((groups, 384, 256), BF16),
        pltpu.VMEM((1024, 256), BF16),
        pltpu.VMEM((1024, 256), BF16),
        pltpu.VMEM((1024, 256), F32),
    ]
    grid_rows = (total_x + 4) * ROWS_X
    if not first:
        scratch += [pltpu.VMEM((grid_rows, 128), F32), pltpu.VMEM((32 * bins, 128), F32)]
    if not last:
        scratch += [pltpu.VMEM((32 * bins, 128), F32), pltpu.VMEM((1024, 128), F32)]
    in_specs = [vmem] * len(operands)
    if not first:
        in_specs[0] = smem
    held = sum(4 * op.size for op in operands) + 512 * grid_rows
    return pl.pallas_call(
        functools.partial(kernel, first, last, bins),
        out_shape=outs,
        in_specs=in_specs,
        out_specs=[vmem] * len(outs),
        scratch_shapes=scratch,
        compiler_params=pltpu.CompilerParams(vmem_limit_bytes=held + (16 << 20)),
    )(*operands)


def column_of(payload):
    count = lax.axis_size("gx")
    if count > 8:
        return lax.all_gather(payload, "gx")
    pieces = [payload]
    for shift in range(1, count):
        pairs = [(i, (i + shift) % count) for i in range(count)]
        pieces.append(lax.ppermute(payload, "gx", pairs))
    return jnp.stack(pieces)


def neighbours_of(column):
    count = lax.axis_size("gy")
    got = []
    for start in range(2):
        pairs = []
        for low in range(start, count - 1, 2):
            pairs += [(low, low + 1), (low + 1, low)]
        got.append(lax.ppermute(column, "gy", pairs) if pairs else jnp.zeros_like(column))
    return got


def shards(
    offsets, cell_index, velocity, affine, strain, particle_mass, owner_row, anchor_xy, anchor_z
):
    bins = offsets.shape[0]
    total_x = TILE * lax.axis_size("gx")
    total_y = TILE * lax.axis_size("gy")
    place_y = lax.axis_index("gy")
    turn = lambda array: jnp.transpose(array, (1, 0, 2))
    corner_x = owner_row[:, 0] * TILE + anchor_xy[:, 0]
    own_row = (corner_x + 2) * ROWS_X + 4 * (anchor_xy[:, 1] + LOW_Y)

    serial = jnp.arange(64, dtype=jnp.int32)[None, :, None]
    group = bins // 16
    spread = lambda values: jnp.repeat(values.reshape(group, 16), 8, axis=1)[:, None, :]
    at_x = spread(corner_x) + serial // 16
    at_y = spread(place_y * TILE + anchor_xy[:, 1]) + serial // 4 % 4
    at_z = spread(anchor_z) + (jnp.arange(128, dtype=jnp.int32) % 8)[None, None, :]
    channel = serial % 4
    at = jnp.where(channel == 1, at_x, jnp.where(channel == 2, at_y, at_z))
    limit = jnp.where(channel == 1, total_x, jnp.where(channel == 2, total_y, CZ))
    in_grid = (at_x >= 0) & (at_x < total_x) & (at_y >= 0) & (at_y < total_y)
    inside = ((at >= 2) & (at < limit - 2) & (channel > 0) & in_grid).astype(F32)

    patch, state = run_kernel(
        True,
        False,
        total_x,
        bins,
        [
            turn(offsets),
            cell_index,
            turn(velocity),
            turn(affine),
            turn(strain),
            particle_mass,
        ],
    )
    facts = jnp.stack(
        [corner_x + 2, anchor_xy[:, 1], anchor_z, jnp.ones((bins,), jnp.int32)]
    ).astype(F32)
    facts = jnp.pad(facts, ((0, 4), (0, 128 - bins)))
    payload = jnp.concatenate([patch, facts], axis=0)
    tabs = None
    for substep in range(SUBSTEPS):
        column = column_of(payload)
        beside = neighbours_of(column)
        if substep == 0:
            even = place_y % 2 == 0
            rows = []
            depths = []
            for at, block in enumerate([column] + beside):
                known = block[:, 4 * bins : 4 * bins + 4, 0:bins].astype(jnp.int32)
                move = (0, jnp.where(even, TILE, -TILE), jnp.where(even, -TILE, TILE))[at]
                y = known[:, 1] + LOW_Y + move
                row = known[:, 0] * ROWS_X + 4 * y
                good = (known[:, 3] > 0) & (y >= 0) & (y <= LOW_Y + TILE + 1)
                rows.append(jnp.where(good, row, -1).reshape(-1))
                depths.append(known[:, 2].reshape(-1))
            tabs = jnp.concatenate([own_row] + rows + [anchor_z] + depths)
        last = substep == SUBSTEPS - 1
        results = run_kernel(
            False, last, total_x, bins, [tabs, column] + beside + [inside, state]
        )
        if not last:
            payload, state = results
    return tuple(turn(array) for array in results)


def solution(mesh):
    wide = P(("runs", "gx", "gy"), None, None)
    flat = P(("runs", "gx", "gy"), None)
    return jax.shard_map(
        shards,
        mesh=mesh,
        in_specs=(wide, flat, wide, wide, wide, flat, flat, flat, P(("runs", "gx", "gy"))),
        out_specs=(wide, wide, wide),
        check_vma=False,
    )
```

```python
import functools

import jax
import jax.numpy as jnp
from jax import lax
from jax.experimental import pallas as pl
from jax.experimental.pallas import tpu as pltpu
from jax.sharding import PartitionSpec as P

TILE = 16
CZ = 128
SUBSTEPS = 4
SPAN_Y = 26
LOW_Y = 5
ROWS_X = 4 * SPAN_Y

time_step = 0.05
shear_coef = 2.0
bulk_coef = 2.0
gravity = 2.0
mass_floor = 0.25

F32 = jnp.float32
BF16 = jnp.bfloat16


def split(value):
    high = value.astype(BF16)
    low = (value - high.astype(F32)).astype(BF16)
    return high, low


def quadratic(f):
    lower = 0.5 * (1.5 - f) ** 2
    middle = 0.75 - (f - 1.0) ** 2
    upper = 0.5 * (f - 0.5) ** 2
    return lower, middle, upper


def row_of(ref, at):
    return jnp.broadcast_to(ref[pl.ds(at, 1), :], (8, 128))


def stencil_rows(group, fractions, bases, params):
    def put(row, value):
        params[pl.ds(group * 128 + row, 8, stride=16), :] = value

    for axis in range(2):
        lower, middle, upper = quadratic(fractions[axis])
        first = bases[axis] < 0.5
        put(4 * axis, jnp.where(first, lower, 0.0))
        put(4 * axis + 1, jnp.where(first, middle, lower))
        put(4 * axis + 2, jnp.where(first, upper, middle))
        put(4 * axis + 3, jnp.where(first, 0.0, upper))
        put(8 + axis, bases[axis] + fractions[axis])
    put(10, fractions[2])
    put(11, bases[2])
    for at, value in enumerate(quadratic(fractions[2])):
        put(12 + at, value)


def depth_weights(bins, params, depth):
    serial = lax.broadcasted_iota(jnp.int32, (8, 128), 0).astype(F32)

    def one(at):
        base = at * 16
        t = serial - row_of(params, base + 11)
        w = jnp.where(
            t == 0.0,
            row_of(params, base + 12),
            jnp.where(
                t == 1.0,
                row_of(params, base + 13),
                jnp.where(t == 2.0, row_of(params, base + 14), 0.0),
            ),
        )
        return jnp.concatenate([w, (t - row_of(params, base + 10)) * w], axis=1)

    def pair(at, _):
        value = jnp.concatenate([one(2 * at), one(2 * at + 1)], axis=0)
        high, low = split(value)
        group = at // 8
        row = pl.multiple_of((at % 8) * 16, 16)
        depth[group, pl.ds(row, 16), :] = high
        depth[group, pl.ds(row + 128, 16), :] = high
        depth[group, pl.ds(row + 256, 16), :] = low
        return _

    lax.fori_loop(0, bins // 2, pair, 0, unroll=4)


def y_patterns(params, base, sub):
    upper_half = sub >= 4
    x1 = row_of(params, base + 9)
    weights = []
    moments = []
    for half in range(2):
        w = jnp.where(
            upper_half, row_of(params, base + 5 + 2 * half), row_of(params, base + 4 + 2 * half)
        )
        j = jnp.where(upper_half, 1.0 + 2 * half, 0.0 + 2 * half)
        weights.append(w)
        moments.append(w * (j - x1))
    return weights, moments


def deposit_rows(group, velocity, affine, deform, mass, blends):
    entries = [[deform[3 * a + b] for b in range(3)] for a in range(3)]
    volume = (
        entries[0][0] * (entries[1][1] * entries[2][2] - entries[1][2] * entries[2][1])
        - entries[0][1] * (entries[1][0] * entries[2][2] - entries[1][2] * entries[2][0])
        + entries[0][2] * (entries[1][0] * entries[2][1] - entries[1][1] * entries[2][0])
    )
    log_volume = jnp.log(volume)

    def put(kind, channel, value):
        for half in range(2):
            blends[pl.ds(group * 256 + kind * 8 + half * 4 + channel, 8, stride=32), :] = value

    zero = jnp.zeros_like(mass)
    put(0, 0, mass)
    for b in range(3):
        put(1 + b, 0, zero)
    for a in range(3):
        put(0, 1 + a, mass * velocity[a])
        for b in range(3):
            product = sum(entries[a][c] * entries[b][c] for c in range(3))
            diagonal = 1.0 if a == b else 0.0
            stress = shear_coef * (product - diagonal) + bulk_coef * log_volume * diagonal
            put(1 + b, 1 + a, mass * affine[3 * a + b] - stress)


def add_patch(sums, row, patch, shift, z, lane):
    moved = pltpu.roll(patch, shift & 127, 1)
    moved = jnp.where((lane >= z) & (lane < z + 8), moved, 0.0)
    for i in range(4):
        place = pl.ds(row + i * ROWS_X, 16)
        sums[place, :] = sums[place, :] + moved[16 * i : 16 * i + 16]


def clear_own(tabs, bins, sums):
    def clear(at, _):
        for i in range(4):
            sums[pl.ds(tabs[at] + i * ROWS_X, 16), :] = jnp.zeros((16, 128), F32)
        return _

    lax.fori_loop(0, bins, clear, 0, unroll=4)


def gather_group(tabs, group, sums, lane):
    total = tabs.shape[0] // 2
    compact = jnp.zeros((64, 128), F32)
    for slot in range(16):
        row = tabs[group * 16 + slot]
        z = tabs[total + group * 16 + slot]
        node = fill([sums[pl.ds(row + i * ROWS_X, 16), :] for i in range(4)])
        moved = pltpu.roll(node, (8 * slot + 128 - z) & 127, 1)
        compact = jnp.where(lane // 8 == slot, moved, compact)
    return compact


def fill(blocks):
    return jnp.concatenate(blocks, axis=0)


def column_kernel(bins, tabs, patch_ref, out, sums):
    lane = lax.broadcasted_iota(jnp.int32, (64, 128), 1)
    total = tabs.shape[0] // 2
    groups = bins // 16
    clear_own(tabs, bins, sums)

    def block(at, _):
        start = pl.multiple_of((at % groups) * 64, 64)
        first = bins + at * 16
        for slot in range(16):
            z = tabs[total + first + slot]
            patch = patch_ref[at // groups, pl.ds(start, 64), :]
            add_patch(sums, tabs[first + slot], patch, z + (128 - 8 * slot), z, lane)
        return _

    lax.fori_loop(0, patch_ref.shape[0] * groups, block, 0)
    for g in range(groups):
        out[g] = gather_group(tabs, g, sums, lane)


def list_bins(tabs, bins, count, listed):
    for side in range(2):

        def one(at, place, side=side):
            listed[side * count + place] = at
            return place + (tabs[bins + side * count + at] >= 0).astype(jnp.int32)

        listed[2 * count + side] = lax.fori_loop(0, count, one, jnp.int32(0), unroll=8)


def scatter_listed(tabs, bins, listed, sides, sums, spare, lane):
    total = tabs.shape[0] // 2
    for side, patch_ref in enumerate(sides):
        count = patch_ref.shape[0] * bins
        many = listed[2 * count + side]

        def some(at, _, side=side, patch_ref=patch_ref, count=count, many=many):
            found = []
            for step in range(4):
                n = at * 4 + step
                used = n < many
                which = listed[side * count + jnp.where(used, n, 0)]
                row = jnp.where(used, tabs[bins + side * count + which], spare)
                z = tabs[total + bins + side * count + which]
                inner = which % bins
                start = pl.multiple_of((inner // 16) * 64, 64)
                patch = patch_ref[which // bins, pl.ds(start, 64), :]
                found.append((row, patch, z + 128 - 8 * (inner % 16), z))
            for row, patch, shift, z in found:
                add_patch(sums, row, patch, shift, z, lane)
            return _

        lax.fori_loop(0, (many + 3) // 4, some, 0)


def kernel(first, listing, last, *refs):
    refs = list(refs)
    take = lambda n: [refs.pop(0) for _ in range(n)]
    if first:
        sources = take(6)
        bins = sources[5].shape[0]
    else:
        (tabs,) = take(1)
        if not listing:
            (listed,) = take(1)
        patch_a, patch_b, compact_in, inside_ref, state_in, params, depth = take(7)
        bins = state_in.shape[1]
    if last:
        velocity_out, affine_out, deform_out = take(3)
    else:
        patch_out, state_out, params_out, depth_out = take(4)
    if listing:
        (listed,) = take(1)
    wide, products = take(2)
    if first:
        held = take(6)
        arrived = refs.pop(0)
        copies = [
            pltpu.make_async_copy(source, target, arrived.at[at])
            for at, (source, target) in enumerate(zip(sources, held))
        ]
        for copy in copies:
            copy.start()
        for copy in copies:
            copy.wait()
        offsets_in, cell, velocity_in, affine_in, strain, mass_in = held
    else:
        sums, results = take(2)
    if not last:
        wide_low, blends, products_low = take(3)
    groups = bins // 16
    sub = lax.broadcasted_iota(jnp.int32, (8, 128), 0)
    lane = lax.broadcasted_iota(jnp.int32, (64, 128), 1)
    lane_row = lax.broadcasted_iota(jnp.int32, (1, 128), 1)

    def load8(g8):
        span = pl.ds(g8 * 8, 8)
        if first:
            fractions = [offsets_in[a, span, :] for a in range(3)]
            c = cell[span, :]
            bx = (c >= 12).astype(jnp.int32)
            c = c - 12 * bx
            by = (c >= 6).astype(jnp.int32)
            bases = [bx.astype(F32), by.astype(F32), (c - 6 * by).astype(F32)]
            deform = [
                strain[e, span, :] + (1.0 if e % 4 == 0 else 0.0) for e in range(9)
            ]
            return fractions, bases, deform, mass_in[span, :]
        fractions = [state_in[a, span, :] for a in range(3)]
        bases = [state_in[3 + a, span, :] for a in range(3)]
        deform = [state_in[7 + e, span, :] for e in range(9)]
        return fractions, bases, deform, state_in[6, span, :]

    def store8(g8, fractions, bases, deform, mass):
        span = pl.ds(g8 * 8, 8)
        for a in range(3):
            state_out[a, span, :] = fractions[a]
            state_out[3 + a, span, :] = bases[a]
        state_out[6, span, :] = mass
        for e in range(9):
            state_out[7 + e, span, :] = deform[e]

    if first:
        for g8 in range(bins // 8):
            span = pl.ds(g8 * 8, 8)
            fractions, bases, deform, mass = load8(g8)
            store8(g8, fractions, bases, deform, mass)
            stencil_rows(g8, fractions, bases, params_out)
            velocity = [velocity_in[a, span, :] for a in range(3)]
            affine = [affine_in[e, span, :] for e in range(9)]
            deposit_rows(g8, velocity, affine, deform, mass, blends)
    else:
        if listing:
            list_bins(tabs, bins, patch_a.shape[0] * bins, listed)
        clear_own(tabs, bins, sums)
        spare = sums.shape[0] - 3 * ROWS_X - 16
        scatter_listed(tabs, bins, listed, [patch_a, patch_b], sums, spare, lane)
        for g in range(groups):
            compact = compact_in[g] + gather_group(tabs, g, sums, lane)
            channel = lax.broadcasted_iota(jnp.int32, (64, 128), 0) & 3
            mass = jnp.where(channel == 0, compact, 0.0)
            mass = mass + pltpu.roll(mass, 1, 0)
            mass = mass + pltpu.roll(mass, 2, 0)
            node = compact / jnp.maximum(mass, mass_floor)
            node = node - jnp.where(channel == 3, time_step * gravity, 0.0)
            node = jnp.where(inside_ref[g] > 0.5, node, 0.0)
            high, low = split(node)
            both = jnp.concatenate([high, low], axis=1)
            for slot in range(16):
                keep = (lane_row // 8 == slot).astype(BF16)
                keep = jnp.concatenate([keep, keep], axis=1)
                wide[64 * slot : 64 * slot + 64, :] = both * keep
            products[...] = jnp.dot(
                wide[...], depth[g, 0:256, :], preferred_element_type=F32
            ) + jnp.dot(wide[:, 0:128], depth[g, 256:384, :], preferred_element_type=F32)

            def finish(slot, _, g=g):
                base = (g * 16 + slot) * 16
                weights, moments = y_patterns(params, base, sub)
                x0 = row_of(params, base + 8)
                at = pl.multiple_of(slot * 64, 64)
                plain = [None, None]
                along = [None, None]
                deep = [None, None]
                for i in range(4):
                    wx = row_of(params, base + i)
                    wxi = wx * (i - x0)
                    for half in range(2):
                        place = pl.ds(at + 16 * i + 8 * half, 8)
                        one = products[place, 0:128]
                        two = products[place, 128:256]
                        terms = (wx * one, wxi * one, wx * two)
                        for kept, term in zip((plain, along, deep), terms):
                            kept[half] = term if i == 0 else kept[half] + term
                found = (
                    weights[0] * plain[0] + weights[1] * plain[1],
                    weights[0] * along[0] + weights[1] * along[1],
                    moments[0] * plain[0] + moments[1] * plain[1],
                    weights[0] * deep[0] + weights[1] * deep[1],
                )
                place = pl.multiple_of((g * 16 + slot) * 32, 32)
                for kind, value in enumerate(found):
                    results[pl.ds(place + 8 * kind, 8), :] = value + pltpu.roll(value, 4, 0)
                return _

            lax.fori_loop(0, 16, finish, 0, unroll=4)

        for g8 in range(bins // 8):
            span = pl.ds(g8 * 8, 8)
            fractions, bases, deform, mass = load8(g8)

            def get(kind, a, g8=g8):
                return results[pl.ds(g8 * 256 + kind * 8 + 1 + a, 8, stride=32), :]

            velocity = [get(0, a) for a in range(3)]
            affine = [4.0 * get(1 + b, a) for a in range(3) for b in range(3)]
            deform = [
                deform[3 * a + b]
                + time_step * sum(affine[3 * a + c] * deform[3 * c + b] for c in range(3))
                for a in range(3)
                for b in range(3)
            ]
            if last:
                for a in range(3):
                    velocity_out[a, span, :] = velocity[a]
                for e in range(9):
                    affine_out[e, span, :] = affine[e]
                    deform_out[e, span, :] = deform[e]
            else:
                fractions = [fractions[a] + time_step * velocity[a] for a in range(3)]
                store8(g8, fractions, bases, deform, mass)
                stencil_rows(g8, fractions, bases, params_out)
                deposit_rows(g8, velocity, affine, deform, mass, blends)

    if not last:
        depth_weights(bins, params_out, depth_out)
        for g in range(groups):

            def build(slot, _, g=g):
                base = (g * 16 + slot) * 16
                place = pl.multiple_of((g * 16 + slot) * 32, 32)
                weights, moments = y_patterns(params_out, base, sub)
                x0 = row_of(params_out, base + 8)
                pushed, b0, b1, b2 = [blends[pl.ds(place + 8 * k, 8), :] for k in range(4)]
                plain = []
                deep = []
                for i in range(4):
                    wx = row_of(params_out, base + i)
                    along = (pushed + b0 * (i - x0)) * wx
                    across = b1 * wx
                    depthwise = b2 * wx
                    for half in range(2):
                        plain.append(along * weights[half] + across * moments[half])
                        deep.append(depthwise * weights[half])
                value = jnp.concatenate([fill(plain), fill(deep)], axis=1)
                high, low = split(value)
                at = pl.ds(pl.multiple_of(slot * 64, 64), 64)
                wide[at, :] = high
                wide_low[at, :] = low
                return _

            lax.fori_loop(0, 16, build, 0, unroll=2)
            turned = (((1,), (1,)), ((), ()))
            products[...] = lax.dot_general(
                wide[...], depth_out[g, 128:384, :], turned, preferred_element_type=F32
            )
            products_low[...] = lax.dot_general(
                wide_low[...], depth_out[g, 128:256, :], turned, preferred_element_type=F32
            )
            compact = jnp.zeros((64, 128), F32)
            for slot in range(16):
                at = slice(64 * slot, 64 * slot + 64)
                value = products[at, 0:128] + products[at, 128:256] + products_low[at, :]
                compact = jnp.where(lane // 8 == slot, value, compact)
            patch_out[64 * g : 64 * g + 64, :] = compact


VMEM_SPEC = pl.BlockSpec(memory_space=pltpu.VMEM)
SMEM_SPEC = pl.BlockSpec(memory_space=pltpu.SMEM)


def shape_of(*dims, dtype=F32):
    return jax.ShapeDtypeStruct(dims, dtype)


def grid_rows(total_x):
    return (total_x + 7) * ROWS_X + 16


def limit_for(operands, total_x):
    held = sum(4 * op.size for op in operands) + 512 * grid_rows(total_x)
    return held + (16 << 20)


def run_column(total_x, bins, tabs, column):
    return pl.pallas_call(
        functools.partial(column_kernel, bins),
        out_shape=shape_of(bins // 16, 64, 128),
        in_specs=[SMEM_SPEC, VMEM_SPEC],
        out_specs=VMEM_SPEC,
        scratch_shapes=[pltpu.VMEM((grid_rows(total_x), 128), F32)],
        cost_estimate=pl.CostEstimate(
            flops=column.size * 10, bytes_accessed=column.size * 160, transcendentals=0
        ),
        compiler_params=pltpu.CompilerParams(vmem_limit_bytes=limit_for([column], total_x)),
    )(tabs, column)


def run_kernel(first, listing, last, total_x, bins, operands):
    if last:
        outs = [shape_of(3, bins, 128), shape_of(9, bins, 128), shape_of(9, bins, 128)]
    else:
        outs = [
            shape_of(4 * bins, 128),
            shape_of(16, bins, 128),
            shape_of(16 * bins, 128),
            shape_of(bins // 16, 384, 256, dtype=BF16),
        ]
    out_specs = [VMEM_SPEC] * len(outs)
    scratch = [pltpu.VMEM((1024, 256), BF16), pltpu.VMEM((1024, 256), F32)]
    in_specs = [VMEM_SPEC] * len(operands)
    if first:
        in_specs = [pl.BlockSpec(memory_space=pl.ANY)] * len(operands)
        scratch += [pltpu.VMEM(op.shape, op.dtype) for op in operands]
        scratch += [pltpu.SemaphoreType.DMA((len(operands),))]
    else:
        in_specs[0] = SMEM_SPEC
        if listing:
            outs.append(shape_of(2 * operands[1].shape[0] * bins + 8, dtype=jnp.int32))
            out_specs.append(SMEM_SPEC)
        else:
            in_specs[1] = SMEM_SPEC
        scratch += [
            pltpu.VMEM((grid_rows(total_x), 128), F32),
            pltpu.VMEM((32 * bins, 128), F32),
        ]
    if not last:
        scratch += [
            pltpu.VMEM((1024, 256), BF16),
            pltpu.VMEM((32 * bins, 128), F32),
            pltpu.VMEM((1024, 128), F32),
        ]
    return pl.pallas_call(
        functools.partial(kernel, first, listing, last),
        out_shape=outs,
        in_specs=in_specs,
        out_specs=out_specs,
        scratch_shapes=scratch,
        compiler_params=pltpu.CompilerParams(vmem_limit_bytes=limit_for(operands, total_x)),
    )(*operands)


def column_of(payload):
    count = lax.axis_size("gx")
    if count > 8:
        return lax.all_gather(payload, "gx")
    pieces = [payload]
    for shift in range(1, count):
        pairs = [(i, (i + shift) % count) for i in range(count)]
        pieces.append(lax.ppermute(payload, "gx", pairs))
    return jnp.stack(pieces)


def neighbours_of(column):
    count = lax.axis_size("gy")
    got = []
    for start in range(2):
        pairs = []
        for low in range(start, count - 1, 2):
            pairs += [(low, low + 1), (low + 1, low)]
        got.append(lax.ppermute(column, "gy", pairs) if pairs else jnp.zeros_like(column))
    return got


def shards(
    offsets, cell_index, velocity, affine, strain, particle_mass, owner_row, anchor_xy, anchor_z
):
    bins = offsets.shape[0]
    total_x = TILE * lax.axis_size("gx")
    total_y = TILE * lax.axis_size("gy")
    place_y = lax.axis_index("gy")
    turn = lambda array: jnp.transpose(array, (1, 0, 2))
    corner_x = owner_row[:, 0] * TILE + anchor_xy[:, 0]
    own_row = (corner_x + 2) * ROWS_X + 4 * (anchor_xy[:, 1] + LOW_Y)

    serial = jnp.arange(64, dtype=jnp.int32)[None, :, None]
    group = bins // 16
    spread = lambda values: jnp.repeat(values.reshape(group, 16), 8, axis=1)[:, None, :]
    at_x = spread(corner_x) + serial // 16
    at_y = spread(place_y * TILE + anchor_xy[:, 1]) + serial // 4 % 4
    at_z = spread(anchor_z) + (jnp.arange(128, dtype=jnp.int32) % 8)[None, None, :]
    channel = serial % 4
    at = jnp.where(channel == 1, at_x, jnp.where(channel == 2, at_y, at_z))
    limit = jnp.where(channel == 1, total_x, jnp.where(channel == 2, total_y, CZ))
    in_grid = (at_x >= 0) & (at_x < total_x) & (at_y >= 0) & (at_y < total_y)
    inside = ((at >= 2) & (at < limit - 2) & (channel > 0) & in_grid).astype(F32)

    patch, state, params, depth = run_kernel(
        True,
        False,
        False,
        total_x,
        bins,
        [
            turn(offsets),
            cell_index,
            turn(velocity),
            turn(affine),
            turn(strain),
            particle_mass,
        ],
    )
    facts = jnp.stack(
        [corner_x + 2, anchor_xy[:, 1], anchor_z, jnp.ones((bins,), jnp.int32)]
    ).astype(F32)
    facts = jnp.pad(facts, ((0, 4), (0, 128 - bins)))
    payload = jnp.concatenate([patch, facts], axis=0)

    def places(block, move):
        known = block[:, 4 * bins : 4 * bins + 4, 0:bins].astype(jnp.int32)
        y = known[:, 1] + LOW_Y + move
        row = known[:, 0] * ROWS_X + 4 * y
        good = (known[:, 3] > 0) & (y >= 0) & (y <= LOW_Y + TILE + 1)
        return jnp.where(good, row, -1).reshape(-1), known[:, 2].reshape(-1)

    step_a = jnp.where(place_y % 2 == 0, TILE, -TILE)
    for substep in range(SUBSTEPS):
        column = column_of(payload)
        beside = neighbours_of(column)
        if substep == 0:
            row, z = places(column, 0)
            column_tabs = jnp.concatenate([own_row, row, anchor_z, z])
            row_a, z_a = places(beside[0], step_a)
            row_b, z_b = places(beside[1], -step_a)
            tabs = jnp.concatenate([own_row, row_a, row_b, anchor_z, z_a, z_b])
        compact = run_column(total_x, bins, column_tabs, column)
        listing = substep == 0
        last = substep == SUBSTEPS - 1
        results = run_kernel(
            False,
            listing,
            last,
            total_x,
            bins,
            [tabs]
            + ([] if listing else [listed])
            + beside
            + [compact, inside, state, params, depth],
        )
        if not last:
            payload, state, params, depth = results[:4]
        if listing:
            listed = results[4]
    return tuple(turn(array) for array in results)


def solution(mesh):
    wide = P(("runs", "gx", "gy"), None, None)
    flat = P(("runs", "gx", "gy"), None)
    return jax.shard_map(
        shards,
        mesh=mesh,
        in_specs=(wide, flat, wide, wide, wide, flat, flat, flat, P(("runs", "gx", "gy"))),
        out_specs=(wide, wide, wide),
        check_vma=False,
    )
```

```python
import functools

import jax
import jax.numpy as jnp
from jax import lax
from jax.experimental import pallas as pl
from jax.experimental.pallas import tpu as pltpu
from jax.sharding import PartitionSpec as P

TILE = 16
CZ = 128
SUBSTEPS = 4
SPAN_Y = 26
LOW_Y = 5
ROWS_X = 4 * SPAN_Y

time_step = 0.05
shear_coef = 2.0
bulk_coef = 2.0
gravity = 2.0
mass_floor = 0.25

F32 = jnp.float32
BF16 = jnp.bfloat16


def split(value):
    high = value.astype(BF16)
    low = (value - high.astype(F32)).astype(BF16)
    return high, low


def quadratic(f):
    lower = 0.5 * (1.5 - f) ** 2
    middle = 0.75 - (f - 1.0) ** 2
    upper = 0.5 * (f - 0.5) ** 2
    return lower, middle, upper


def row_of(ref, at):
    return jnp.broadcast_to(ref[pl.ds(at, 1), :], (8, 128))


def stencil_rows(group, fractions, bases, params):
    def put(row, value):
        params[pl.ds(group * 128 + row, 8, stride=16), :] = value

    for axis in range(2):
        lower, middle, upper = quadratic(fractions[axis])
        first = bases[axis] < 0.5
        put(4 * axis, jnp.where(first, lower, 0.0))
        put(4 * axis + 1, jnp.where(first, middle, lower))
        put(4 * axis + 2, jnp.where(first, upper, middle))
        put(4 * axis + 3, jnp.where(first, 0.0, upper))
        put(8 + axis, bases[axis] + fractions[axis])
    put(10, fractions[2])
    put(11, bases[2])
    for at, value in enumerate(quadratic(fractions[2])):
        put(12 + at, value)


def depth_weights(bins, params, depth):
    serial = lax.broadcasted_iota(jnp.int32, (8, 128), 0).astype(F32)

    def one(at):
        base = at * 16
        t = serial - row_of(params, base + 11)
        w = jnp.where(
            t == 0.0,
            row_of(params, base + 12),
            jnp.where(
                t == 1.0,
                row_of(params, base + 13),
                jnp.where(t == 2.0, row_of(params, base + 14), 0.0),
            ),
        )
        return jnp.concatenate([w, (t - row_of(params, base + 10)) * w], axis=1)

    def pair(at, _):
        value = jnp.concatenate([one(2 * at), one(2 * at + 1)], axis=0)
        high, low = split(value)
        group = at // 8
        row = pl.multiple_of((at % 8) * 16, 16)
        depth[group, pl.ds(row, 16), :] = high
        depth[group, pl.ds(row + 128, 16), :] = high
        depth[group, pl.ds(row + 256, 16), :] = low
        return _

    lax.fori_loop(0, bins // 2, pair, 0, unroll=4)


def y_patterns(params, base, sub):
    upper_half = sub >= 4
    x1 = row_of(params, base + 9)
    weights = []
    moments = []
    for half in range(2):
        w = jnp.where(
            upper_half, row_of(params, base + 5 + 2 * half), row_of(params, base + 4 + 2 * half)
        )
        j = jnp.where(upper_half, 1.0 + 2 * half, 0.0 + 2 * half)
        weights.append(w)
        moments.append(w * (j - x1))
    return weights, moments


def deposit_rows(group, velocity, affine, deform, mass, blends):
    entries = [[deform[3 * a + b] for b in range(3)] for a in range(3)]
    volume = (
        entries[0][0] * (entries[1][1] * entries[2][2] - entries[1][2] * entries[2][1])
        - entries[0][1] * (entries[1][0] * entries[2][2] - entries[1][2] * entries[2][0])
        + entries[0][2] * (entries[1][0] * entries[2][1] - entries[1][1] * entries[2][0])
    )
    log_volume = jnp.log(volume)

    def put(kind, channel, value):
        for half in range(2):
            blends[pl.ds(group * 256 + kind * 8 + half * 4 + channel, 8, stride=32), :] = value

    zero = jnp.zeros_like(mass)
    put(0, 0, mass)
    for b in range(3):
        put(1 + b, 0, zero)
    for a in range(3):
        put(0, 1 + a, mass * velocity[a])
        for b in range(3):
            product = sum(entries[a][c] * entries[b][c] for c in range(3))
            diagonal = 1.0 if a == b else 0.0
            stress = shear_coef * (product - diagonal) + bulk_coef * log_volume * diagonal
            put(1 + b, 1 + a, mass * affine[3 * a + b] - stress)


def add_patch(sums, row, patch, shift, z, lane):
    moved = pltpu.roll(patch, shift & 127, 1)
    moved = jnp.where((lane >= z) & (lane < z + 8), moved, 0.0)
    for i in range(4):
        place = pl.ds(row + i * ROWS_X, 16)
        sums[place, :] = sums[place, :] + moved[16 * i : 16 * i + 16]


def clear_own(tabs, bins, sums):
    def clear(at, _):
        for i in range(4):
            sums[pl.ds(tabs[at] + i * ROWS_X, 16), :] = jnp.zeros((16, 128), F32)
        return _

    lax.fori_loop(0, bins, clear, 0, unroll=4)


def gather_group(tabs, group, sums, lane):
    total = tabs.shape[0] // 2
    compact = jnp.zeros((64, 128), F32)
    for slot in range(16):
        row = tabs[group * 16 + slot]
        z = tabs[total + group * 16 + slot]
        node = fill([sums[pl.ds(row + i * ROWS_X, 16), :] for i in range(4)])
        moved = pltpu.roll(node, (8 * slot + 128 - z) & 127, 1)
        compact = jnp.where(lane // 8 == slot, moved, compact)
    return compact


def fill(blocks):
    return jnp.concatenate(blocks, axis=0)


def column_kernel(bins, tabs, patch_ref, out, sums):
    lane = lax.broadcasted_iota(jnp.int32, (64, 128), 1)
    total = tabs.shape[0] // 2
    groups = bins // 16
    clear_own(tabs, bins, sums)

    def block(at, _):
        start = pl.multiple_of((at % groups) * 64, 64)
        first = bins + at * 16
        for slot in range(16):
            z = tabs[total + first + slot]
            patch = patch_ref[at // groups, pl.ds(start, 64), :]
            add_patch(sums, tabs[first + slot], patch, z + (128 - 8 * slot), z, lane)
        return _

    lax.fori_loop(0, patch_ref.shape[0] * groups, block, 0)
    for g in range(groups):
        out[g] = gather_group(tabs, g, sums, lane)


def list_bins(tabs, bins, count, listed):
    for side in range(2):

        def one(at, place, side=side):
            listed[side * count + place] = at
            return place + (tabs[bins + side * count + at] >= 0).astype(jnp.int32)

        listed[2 * count + side] = lax.fori_loop(0, count, one, jnp.int32(0), unroll=8)


def scatter_listed(tabs, bins, listed, sides, sums, spare, lane):
    total = tabs.shape[0] // 2
    count = sides[0].shape[0] * bins
    many = [listed[2 * count + side] for side in range(2)]

    def some(at, _):
        found = []
        for step in range(8):
            n = at * 8 + step
            for side, patch_ref in enumerate(sides):
                used = n < many[side]
                which = listed[side * count + jnp.where(used, n, 0)]
                which = jnp.where(used, which, 0)
                place = bins + side * count + which
                row = jnp.where(used, tabs[place], spare)
                z = tabs[total + place]
                inner = which % bins
                start = pl.multiple_of((inner // 16) * 64, 64)
                patch = patch_ref[which // bins, pl.ds(start, 64), :]
                found.append((row, patch, z + 128 - 8 * (inner % 16), z))
        for row, patch, shift, z in found:
            add_patch(sums, row, patch, shift, z, lane)
        return _

    lax.fori_loop(0, (jnp.maximum(many[0], many[1]) + 7) // 8, some, 0)


def kernel(first, listing, last, *refs):
    refs = list(refs)
    take = lambda n: [refs.pop(0) for _ in range(n)]
    if first:
        sources = take(9)
        bins = sources[5].shape[0]
    else:
        (tabs,) = take(1)
        if not listing:
            (listed,) = take(1)
        patch_a, patch_b, compact_in, inside_ref, state_in, params, depth = take(7)
        bins = state_in.shape[1]
    if last:
        velocity_out, affine_out, deform_out = take(3)
    else:
        patch_out, state_out, params_out, depth_out = take(4)
    if listing:
        (listed,) = take(1)
    wides, products_all = take(2)
    if first:
        held = take(9)
        arrived = refs.pop(0)
        copies = [
            pltpu.make_async_copy(source, target, arrived.at[at])
            for at, (source, target) in enumerate(zip(sources, held))
        ]
        for copy in copies:
            copy.start()
        for copy in copies:
            copy.wait()
        offsets_in, cell, velocity_in, affine_in, strain, mass_in, owner, corner, depth_at = held
        facts = slice(4 * bins, 4 * bins + 8)
        patch_out[facts, :] = jnp.zeros((8, 128), F32)
        known = (owner[...] * TILE + corner[0:1, :] + 2, corner[1:2, :], depth_at[...])
        for at, value in enumerate(known):
            patch_out[4 * bins + at : 4 * bins + at + 1, 0:bins] = value.astype(F32)
        patch_out[4 * bins + 3 : 4 * bins + 4, 0:bins] = jnp.ones((1, bins), F32)
    else:
        sums, results = take(2)
    if not last:
        wides_low, blends, products_lows = take(3)
    groups = bins // 16
    sub = lax.broadcasted_iota(jnp.int32, (8, 128), 0)
    lane = lax.broadcasted_iota(jnp.int32, (64, 128), 1)
    lane_row = lax.broadcasted_iota(jnp.int32, (1, 128), 1)

    def load8(g8):
        span = pl.ds(g8 * 8, 8)
        if first:
            fractions = [offsets_in[a, span, :] for a in range(3)]
            c = cell[span, :]
            bx = (c >= 12).astype(jnp.int32)
            c = c - 12 * bx
            by = (c >= 6).astype(jnp.int32)
            bases = [bx.astype(F32), by.astype(F32), (c - 6 * by).astype(F32)]
            deform = [
                strain[e, span, :] + (1.0 if e % 4 == 0 else 0.0) for e in range(9)
            ]
            return fractions, bases, deform, mass_in[span, :]
        fractions = [state_in[a, span, :] for a in range(3)]
        bases = [state_in[3 + a, span, :] for a in range(3)]
        deform = [state_in[7 + e, span, :] for e in range(9)]
        return fractions, bases, deform, state_in[6, span, :]

    def store8(g8, fractions, bases, deform, mass):
        span = pl.ds(g8 * 8, 8)
        for a in range(3):
            state_out[a, span, :] = fractions[a]
            state_out[3 + a, span, :] = bases[a]
        state_out[6, span, :] = mass
        for e in range(9):
            state_out[7 + e, span, :] = deform[e]

    if first:
        for g8 in range(bins // 8):
            span = pl.ds(g8 * 8, 8)
            fractions, bases, deform, mass = load8(g8)
            store8(g8, fractions, bases, deform, mass)
            stencil_rows(g8, fractions, bases, params_out)
            velocity = [velocity_in[a, span, :] for a in range(3)]
            affine = [affine_in[e, span, :] for e in range(9)]
            deposit_rows(g8, velocity, affine, deform, mass, blends)
    else:
        if listing:
            list_bins(tabs, bins, patch_a.shape[0] * bins, listed)
        clear_own(tabs, bins, sums)
        spare = sums.shape[0] - 3 * ROWS_X - 16
        scatter_listed(tabs, bins, listed, [patch_a, patch_b], sums, spare, lane)
        for g in range(groups):
            compact = compact_in[g] + gather_group(tabs, g, sums, lane)
            wide, products = wides.at[g], products_all.at[g]
            channel = lax.broadcasted_iota(jnp.int32, (64, 128), 0) & 3
            mass = jnp.where(channel == 0, compact, 0.0)
            mass = mass + pltpu.roll(mass, 1, 0)
            mass = mass + pltpu.roll(mass, 2, 0)
            node = compact / jnp.maximum(mass, mass_floor)
            node = node - jnp.where(channel == 3, time_step * gravity, 0.0)
            node = jnp.where(inside_ref[g] > 0.5, node, 0.0)
            high, low = split(node)
            both = jnp.concatenate([high, low], axis=1)
            for slot in range(16):
                keep = (lane_row // 8 == slot).astype(BF16)
                keep = jnp.concatenate([keep, keep], axis=1)
                wide[64 * slot : 64 * slot + 64, :] = both * keep
            products[...] = jnp.dot(
                wide[...], depth[g, 0:256, :], preferred_element_type=F32
            ) + jnp.dot(wide[:, 0:128], depth[g, 256:384, :], preferred_element_type=F32)

            def finish(slot, _, g=g, products=products):
                base = (g * 16 + slot) * 16
                weights, moments = y_patterns(params, base, sub)
                x0 = row_of(params, base + 8)
                at = slot * 64
                plain = [None, None]
                along = [None, None]
                deep = [None, None]
                for i in range(4):
                    wx = row_of(params, base + i)
                    wxi = wx * (i - x0)
                    for half in range(2):
                        place = pl.ds(at + 16 * i + 8 * half, 8)
                        one = products[place, 0:128]
                        two = products[place, 128:256]
                        terms = (wx * one, wxi * one, wx * two)
                        for kept, term in zip((plain, along, deep), terms):
                            kept[half] = term if i == 0 else kept[half] + term
                found = (
                    weights[0] * plain[0] + weights[1] * plain[1],
                    weights[0] * along[0] + weights[1] * along[1],
                    moments[0] * plain[0] + moments[1] * plain[1],
                    weights[0] * deep[0] + weights[1] * deep[1],
                )
                place = (g * 16 + slot) * 32
                for kind, value in enumerate(found):
                    results[pl.ds(place + 8 * kind, 8), :] = value + pltpu.roll(value, 4, 0)
                return _

            for slot in range(16):
                finish(slot, 0)

        for g8 in range(bins // 8):
            span = pl.ds(g8 * 8, 8)
            fractions, bases, deform, mass = load8(g8)

            def get(kind, a, g8=g8):
                return results[pl.ds(g8 * 256 + kind * 8 + 1 + a, 8, stride=32), :]

            velocity = [get(0, a) for a in range(3)]
            affine = [4.0 * get(1 + b, a) for a in range(3) for b in range(3)]
            deform = [
                deform[3 * a + b]
                + time_step * sum(affine[3 * a + c] * deform[3 * c + b] for c in range(3))
                for a in range(3)
                for b in range(3)
            ]
            if last:
                for a in range(3):
                    velocity_out[a, span, :] = velocity[a]
                for e in range(9):
                    affine_out[e, span, :] = affine[e]
                    deform_out[e, span, :] = deform[e]
            else:
                fractions = [fractions[a] + time_step * velocity[a] for a in range(3)]
                store8(g8, fractions, bases, deform, mass)
                stencil_rows(g8, fractions, bases, params_out)
                deposit_rows(g8, velocity, affine, deform, mass, blends)

    if not last:
        depth_weights(bins, params_out, depth_out)
        for g in range(groups):
            wide, wide_low = wides.at[g], wides_low.at[g]
            products, products_low = products_all.at[g], products_lows.at[g]

            def build(slot, _, g=g, wide=wide, wide_low=wide_low):
                base = (g * 16 + slot) * 16
                place = (g * 16 + slot) * 32
                weights, moments = y_patterns(params_out, base, sub)
                x0 = row_of(params_out, base + 8)
                pushed, b0, b1, b2 = [blends[pl.ds(place + 8 * k, 8), :] for k in range(4)]
                plain = []
                deep = []
                for i in range(4):
                    wx = row_of(params_out, base + i)
                    along = (pushed + b0 * (i - x0)) * wx
                    across = b1 * wx
                    depthwise = b2 * wx
                    for half in range(2):
                        plain.append(along * weights[half] + across * moments[half])
                        deep.append(depthwise * weights[half])
                value = jnp.concatenate([fill(plain), fill(deep)], axis=1)
                high, low = split(value)
                at = pl.ds(slot * 64, 64)
                wide[at, :] = high
                wide_low[at, :] = low
                return _

            for slot in range(16):
                build(slot, 0)
            turned = (((1,), (1,)), ((), ()))
            products[...] = lax.dot_general(
                wide[...], depth_out[g, 128:384, :], turned, preferred_element_type=F32
            )
            products_low[...] = lax.dot_general(
                wide_low[...], depth_out[g, 128:256, :], turned, preferred_element_type=F32
            )
            compact = jnp.zeros((64, 128), F32)
            for slot in range(16):
                at = slice(64 * slot, 64 * slot + 64)
                value = products[at, 0:128] + products[at, 128:256] + products_low[at, :]
                compact = jnp.where(lane // 8 == slot, value, compact)
            patch_out[64 * g : 64 * g + 64, :] = compact


VMEM_SPEC = pl.BlockSpec(memory_space=pltpu.VMEM)
SMEM_SPEC = pl.BlockSpec(memory_space=pltpu.SMEM)


def shape_of(*dims, dtype=F32):
    return jax.ShapeDtypeStruct(dims, dtype)


def grid_rows(total_x):
    return (total_x + 7) * ROWS_X + 16


def limit_for(operands, total_x):
    held = sum(4 * op.size for op in operands) + 512 * grid_rows(total_x)
    return held + (16 << 20)


def run_column(total_x, bins, tabs, column):
    return pl.pallas_call(
        functools.partial(column_kernel, bins),
        out_shape=shape_of(bins // 16, 64, 128),
        in_specs=[SMEM_SPEC, VMEM_SPEC],
        out_specs=VMEM_SPEC,
        scratch_shapes=[pltpu.VMEM((grid_rows(total_x), 128), F32)],
        cost_estimate=pl.CostEstimate(
            flops=column.size * 10, bytes_accessed=column.size * 160, transcendentals=0
        ),
        compiler_params=pltpu.CompilerParams(vmem_limit_bytes=limit_for([column], total_x)),
    )(tabs, column)


def run_kernel(first, listing, last, total_x, bins, operands):
    if last:
        outs = [shape_of(3, bins, 128), shape_of(9, bins, 128), shape_of(9, bins, 128)]
    else:
        outs = [
            shape_of(4 * bins + (8 if first else 0), 128),
            shape_of(16, bins, 128),
            shape_of(16 * bins, 128),
            shape_of(bins // 16, 384, 256, dtype=BF16),
        ]
    out_specs = [VMEM_SPEC] * len(outs)
    scratch = [
        pltpu.VMEM((bins // 16, 1024, 256), BF16),
        pltpu.VMEM((bins // 16, 1024, 256), F32),
    ]
    in_specs = [VMEM_SPEC] * len(operands)
    if first:
        in_specs = [pl.BlockSpec(memory_space=pltpu.HBM)] * len(operands)
        scratch += [pltpu.VMEM(op.shape, op.dtype) for op in operands]
        scratch += [pltpu.SemaphoreType.DMA((len(operands),))]
    else:
        in_specs[0] = SMEM_SPEC
        if listing:
            outs.append(shape_of(2 * operands[1].shape[0] * bins + 8, dtype=jnp.int32))
            out_specs.append(SMEM_SPEC)
        else:
            in_specs[1] = SMEM_SPEC
        scratch += [
            pltpu.VMEM((grid_rows(total_x), 128), F32),
            pltpu.VMEM((32 * bins, 128), F32),
        ]
    if not last:
        scratch += [
            pltpu.VMEM((bins // 16, 1024, 256), BF16),
            pltpu.VMEM((32 * bins, 128), F32),
            pltpu.VMEM((bins // 16, 1024, 128), F32),
        ]
    if first:
        operands = [pltpu.with_memory_space_constraint(op, pltpu.HBM) for op in operands]
    return pl.pallas_call(
        functools.partial(kernel, first, listing, last),
        out_shape=outs,
        in_specs=in_specs,
        out_specs=out_specs,
        scratch_shapes=scratch,
        compiler_params=pltpu.CompilerParams(vmem_limit_bytes=limit_for(operands, total_x)),
    )(*operands)


def column_of(payload):
    count = lax.axis_size("gx")
    if count > 8:
        return lax.all_gather(payload, "gx")
    pieces = [payload]
    for shift in range(1, count):
        pairs = [(i, (i + shift) % count) for i in range(count)]
        pieces.append(lax.ppermute(payload, "gx", pairs))
    return jnp.stack(pieces)


def neighbours_of(column):
    count = lax.axis_size("gy")
    got = []
    for start in range(2):
        pairs = []
        for low in range(start, count - 1, 2):
            pairs += [(low, low + 1), (low + 1, low)]
        got.append(lax.ppermute(column, "gy", pairs) if pairs else jnp.zeros_like(column))
    return got


def shards(
    offsets, cell_index, velocity, affine, strain, particle_mass, owner_row, anchor_xy, anchor_z
):
    bins = offsets.shape[0]
    total_x = TILE * lax.axis_size("gx")
    total_y = TILE * lax.axis_size("gy")
    place_y = lax.axis_index("gy")
    turn = lambda array: jnp.transpose(array, (1, 0, 2))
    payload, state, params, depth = run_kernel(
        True,
        False,
        False,
        total_x,
        bins,
        [
            turn(offsets),
            cell_index,
            turn(velocity),
            turn(affine),
            turn(strain),
            particle_mass,
            owner_row.T,
            anchor_xy.T,
            anchor_z[None, :],
        ],
    )
    def inside_grid(late_x, late_y, late_z):
        serial = jnp.arange(64, dtype=jnp.int32)[None, :, None]
        group = bins // 16
        spread = lambda values: jnp.repeat(values.reshape(group, 16), 8, axis=1)[:, None, :]
        at_x = spread(late_x) + serial // 16
        at_y = spread(place_y * TILE + late_y) + serial // 4 % 4
        at_z = spread(late_z) + (jnp.arange(128, dtype=jnp.int32) % 8)[None, None, :]
        channel = serial % 4
        at = jnp.where(channel == 1, at_x, jnp.where(channel == 2, at_y, at_z))
        limit = jnp.where(channel == 1, total_x, jnp.where(channel == 2, total_y, CZ))
        in_grid = (at_x >= 0) & (at_x < total_x) & (at_y >= 0) & (at_y < total_y)
        inside = ((at >= 2) & (at < limit - 2) & (channel > 0) & in_grid).astype(F32)
        return inside

    def places(block, move):
        known = block[:, 4 * bins : 4 * bins + 4, 0:bins].astype(jnp.int32)
        y = known[:, 1] + LOW_Y + move
        row = known[:, 0] * ROWS_X + 4 * y
        good = (known[:, 3] > 0) & (y >= 0) & (y <= LOW_Y + TILE + 1)
        return jnp.where(good, row, -1).reshape(-1), known[:, 2].reshape(-1)

    step_a = jnp.where(place_y % 2 == 0, TILE, -TILE)
    for substep in range(SUBSTEPS):
        column = column_of(payload)
        beside = neighbours_of(column)
        if substep == 0:
            own = payload[4 * bins : 4 * bins + 3, 0:bins].astype(jnp.int32)
            own_row = own[0] * ROWS_X + 4 * (own[1] + LOW_Y)
            anchor_z = own[2]
            late, _ = lax.optimization_barrier((payload[4 * bins : 4 * bins + 3], column))
            late = late[:, 0:bins].astype(jnp.int32)
            inside = inside_grid(late[0] - 2, late[1], late[2])
            row, z = places(column, 0)
            column_tabs = jnp.concatenate([own_row, row, anchor_z, z])
            row_a, z_a = places(beside[0], step_a)
            row_b, z_b = places(beside[1], -step_a)
            tabs = jnp.concatenate([own_row, row_a, row_b, anchor_z, z_a, z_b])
        compact = run_column(total_x, bins, column_tabs, column)
        listing = substep == 0
        last = substep == SUBSTEPS - 1
        results = run_kernel(
            False,
            listing,
            last,
            total_x,
            bins,
            [tabs]
            + ([] if listing else [listed])
            + beside
            + [compact, inside, state, params, depth],
        )
        if not last:
            payload, state, params, depth = results[:4]
        if listing:
            listed = results[4]
    return tuple(turn(array) for array in results)


def solution(mesh):
    wide = P(("runs", "gx", "gy"), None, None)
    flat = P(("runs", "gx", "gy"), None)
    return jax.shard_map(
        shards,
        mesh=mesh,
        in_specs=(wide, flat, wide, wide, wide, flat, flat, flat, P(("runs", "gx", "gy"))),
        out_specs=(wide, wide, wide),
        check_vma=False,
    )
```

```python
import functools

import jax
import jax.numpy as jnp
from jax import lax
from jax.experimental import pallas as pl
from jax.experimental.pallas import tpu as pltpu
from jax.sharding import PartitionSpec as P

TILE = 16
CZ = 128
SUBSTEPS = 4
SPAN_Y = 26
LOW_Y = 5
ROWS_X = 4 * SPAN_Y

time_step = 0.05
shear_coef = 2.0
bulk_coef = 2.0
gravity = 2.0
mass_floor = 0.25

F32 = jnp.float32
BF16 = jnp.bfloat16


def split(value):
    high = value.astype(BF16)
    low = (value - high.astype(F32)).astype(BF16)
    return high, low


def quadratic(f):
    lower = 0.5 * (1.5 - f) ** 2
    middle = 0.75 - (f - 1.0) ** 2
    upper = 0.5 * (f - 0.5) ** 2
    return lower, middle, upper


def row_of(ref, at):
    return jnp.broadcast_to(ref[pl.ds(at, 1), :], (8, 128))


def stencil_rows(group, fractions, bases, params):
    def put(row, value):
        params[pl.ds(group * 128 + row, 8, stride=16), :] = value

    for axis in range(2):
        lower, middle, upper = quadratic(fractions[axis])
        first = bases[axis] < 0.5
        put(4 * axis, jnp.where(first, lower, 0.0))
        put(4 * axis + 1, jnp.where(first, middle, lower))
        put(4 * axis + 2, jnp.where(first, upper, middle))
        put(4 * axis + 3, jnp.where(first, 0.0, upper))
        put(8 + axis, bases[axis] + fractions[axis])
    put(10, fractions[2])
    put(11, bases[2])
    for at, value in enumerate(quadratic(fractions[2])):
        put(12 + at, value)


def depth_weights(group, params, depth):
    serial = lax.broadcasted_iota(jnp.int32, (8, 128), 0).astype(F32)

    def one(at):
        base = at * 16
        t = serial - row_of(params, base + 11)
        w = jnp.where(
            t == 0.0,
            row_of(params, base + 12),
            jnp.where(
                t == 1.0,
                row_of(params, base + 13),
                jnp.where(t == 2.0, row_of(params, base + 14), 0.0),
            ),
        )
        return jnp.concatenate([w, (t - row_of(params, base + 10)) * w], axis=1)

    for pair in range(8):
        at = 16 * group + 2 * pair
        high, low = split(jnp.concatenate([one(at), one(at + 1)], axis=0))
        row = 16 * pair
        depth[group, row : row + 16, :] = high
        depth[group, row + 128 : row + 144, :] = high
        depth[group, row + 256 : row + 272, :] = low


def y_patterns(params, base, sub):
    upper_half = sub >= 4
    x1 = row_of(params, base + 9)
    weights = []
    moments = []
    for half in range(2):
        w = jnp.where(
            upper_half, row_of(params, base + 5 + 2 * half), row_of(params, base + 4 + 2 * half)
        )
        j = jnp.where(upper_half, 1.0 + 2 * half, 0.0 + 2 * half)
        weights.append(w)
        moments.append(w * (j - x1))
    return weights, moments


def deposit_rows(group, velocity, affine, deform, mass, blends):
    entries = [[deform[3 * a + b] for b in range(3)] for a in range(3)]
    volume = (
        entries[0][0] * (entries[1][1] * entries[2][2] - entries[1][2] * entries[2][1])
        - entries[0][1] * (entries[1][0] * entries[2][2] - entries[1][2] * entries[2][0])
        + entries[0][2] * (entries[1][0] * entries[2][1] - entries[1][1] * entries[2][0])
    )
    log_volume = jnp.log(volume)

    def put(kind, channel, value):
        for half in range(2):
            blends[pl.ds(group * 256 + kind * 8 + half * 4 + channel, 8, stride=32), :] = value

    zero = jnp.zeros_like(mass)
    put(0, 0, mass)
    for b in range(3):
        put(1 + b, 0, zero)
    for a in range(3):
        put(0, 1 + a, mass * velocity[a])
        for b in range(3):
            product = sum(entries[a][c] * entries[b][c] for c in range(3))
            diagonal = 1.0 if a == b else 0.0
            stress = shear_coef * (product - diagonal) + bulk_coef * log_volume * diagonal
            put(1 + b, 1 + a, mass * affine[3 * a + b] - stress)


def add_patch(sums, row, patch, shift, z, lane):
    moved = pltpu.roll(patch, shift & 127, 1)
    moved = jnp.where((lane >= z) & (lane < z + 8), moved, 0.0)
    for i in range(4):
        place = pl.ds(row + i * ROWS_X, 16)
        sums[place, :] = sums[place, :] + moved[16 * i : 16 * i + 16]


def clear_own(tabs, bins, sums):
    for at in range(bins):
        for i in range(4):
            sums[pl.ds(tabs[at] + i * ROWS_X, 16), :] = jnp.zeros((16, 128), F32)


def gather_group(tabs, group, sums, lane):
    total = tabs.shape[0] // 2
    compact = jnp.zeros((64, 128), F32)
    for slot in range(16):
        row = tabs[group * 16 + slot]
        z = tabs[total + group * 16 + slot]
        node = fill([sums[pl.ds(row + i * ROWS_X, 16), :] for i in range(4)])
        moved = pltpu.roll(node, (8 * slot + 128 - z) & 127, 1)
        compact = jnp.where(lane // 8 == slot, moved, compact)
    return compact


def fill(blocks):
    return jnp.concatenate(blocks, axis=0)


def column_kernel(bins, tabs, patch_ref, out, sums):
    lane = lax.broadcasted_iota(jnp.int32, (64, 128), 1)
    total = tabs.shape[0] // 2
    groups = bins // 16
    clear_own(tabs, bins, sums)

    def block(at, _):
        start = pl.multiple_of((at % groups) * 64, 64)
        first = bins + at * 16
        for slot in range(16):
            z = tabs[total + first + slot]
            patch = patch_ref[at // groups, pl.ds(start, 64), :]
            add_patch(sums, tabs[first + slot], patch, z + (128 - 8 * slot), z, lane)
        return _

    lax.fori_loop(0, patch_ref.shape[0] * groups, block, 0)
    for g in range(groups):
        out[g] = gather_group(tabs, g, sums, lane)


def list_bins(tabs, bins, count, listed):
    for side in range(2):

        def one(at, place, side=side):
            listed[side * count + place] = at
            return place + (tabs[bins + side * count + at] >= 0).astype(jnp.int32)

        listed[2 * count + side] = lax.fori_loop(0, count, one, jnp.int32(0), unroll=8)


def scatter_listed(tabs, bins, listed, sides, sums, spare, lane):
    total = tabs.shape[0] // 2
    count = sides[0].shape[0] * bins
    many = [listed[2 * count + side] for side in range(2)]

    def some(at, _):
        found = []
        for step in range(8):
            n = at * 8 + step
            for side, patch_ref in enumerate(sides):
                used = n < many[side]
                which = listed[side * count + jnp.where(used, n, 0)]
                which = jnp.where(used, which, 0)
                place = bins + side * count + which
                row = jnp.where(used, tabs[place], spare)
                z = tabs[total + place]
                inner = which % bins
                start = pl.multiple_of((inner // 16) * 64, 64)
                patch = patch_ref[which // bins, pl.ds(start, 64), :]
                found.append((row, patch, z + 128 - 8 * (inner % 16), z))
        for row, patch, shift, z in found:
            add_patch(sums, row, patch, shift, z, lane)
        return _

    lax.fori_loop(0, (jnp.maximum(many[0], many[1]) + 7) // 8, some, 0)


def kernel(first, listing, last, *refs):
    refs = list(refs)
    take = lambda n: [refs.pop(0) for _ in range(n)]
    if first:
        sources = take(9)
        bins = sources[5].shape[0]
    else:
        (tabs,) = take(1)
        if not listing:
            (listed,) = take(1)
        patch_a, patch_b, compact_in, inside_ref, state_in, params, depth = take(7)
        bins = state_in.shape[1]
    if last:
        velocity_out, affine_out, deform_out = take(3)
    else:
        patch_out, state_out, params_out, depth_out = take(4)
    if listing:
        (listed,) = take(1)
    wides, products_all = take(2)
    if first:
        held = take(9)
        arrived = refs.pop(0)
        copies = [
            pltpu.make_async_copy(source, target, arrived.at[at])
            for at, (source, target) in enumerate(zip(sources, held))
        ]
        for copy in copies:
            copy.start()
        for copy in copies:
            copy.wait()
        offsets_in, cell, velocity_in, affine_in, strain, mass_in, owner, corner, depth_at = held
        facts = slice(4 * bins, 4 * bins + 8)
        patch_out[facts, :] = jnp.zeros((8, 128), F32)
        known = (owner[...] * TILE + corner[0:1, :] + 2, corner[1:2, :], depth_at[...])
        for at, value in enumerate(known):
            patch_out[4 * bins + at : 4 * bins + at + 1, 0:bins] = value.astype(F32)
        patch_out[4 * bins + 3 : 4 * bins + 4, 0:bins] = jnp.ones((1, bins), F32)
    else:
        sums, results = take(2)
    if not last:
        wides_low, blends, products_lows = take(3)
    groups = bins // 16
    sub = lax.broadcasted_iota(jnp.int32, (8, 128), 0)
    lane = lax.broadcasted_iota(jnp.int32, (64, 128), 1)
    lane_row = lax.broadcasted_iota(jnp.int32, (1, 128), 1)

    def load8(g8):
        span = pl.ds(g8 * 8, 8)
        if first:
            fractions = [offsets_in[a, span, :] for a in range(3)]
            c = cell[span, :]
            bx = (c >= 12).astype(jnp.int32)
            c = c - 12 * bx
            by = (c >= 6).astype(jnp.int32)
            bases = [bx.astype(F32), by.astype(F32), (c - 6 * by).astype(F32)]
            deform = [
                strain[e, span, :] + (1.0 if e % 4 == 0 else 0.0) for e in range(9)
            ]
            return fractions, bases, deform, mass_in[span, :]
        fractions = [state_in[a, span, :] for a in range(3)]
        bases = [state_in[3 + a, span, :] for a in range(3)]
        deform = [state_in[7 + e, span, :] for e in range(9)]
        return fractions, bases, deform, state_in[6, span, :]

    def store8(g8, fractions, bases, deform, mass):
        span = pl.ds(g8 * 8, 8)
        for a in range(3):
            state_out[a, span, :] = fractions[a]
            state_out[3 + a, span, :] = bases[a]
        state_out[6, span, :] = mass
        for e in range(9):
            state_out[7 + e, span, :] = deform[e]

    if first:
        for g8 in range(bins // 8):
            span = pl.ds(g8 * 8, 8)
            fractions, bases, deform, mass = load8(g8)
            store8(g8, fractions, bases, deform, mass)
            stencil_rows(g8, fractions, bases, params_out)
            velocity = [velocity_in[a, span, :] for a in range(3)]
            affine = [affine_in[e, span, :] for e in range(9)]
            deposit_rows(g8, velocity, affine, deform, mass, blends)
    else:
        if listing:
            list_bins(tabs, bins, patch_a.shape[0] * bins, listed)
        clear_own(tabs, bins, sums)
        spare = sums.shape[0] - 3 * ROWS_X - 16
        scatter_listed(tabs, bins, listed, [patch_a, patch_b], sums, spare, lane)
        for g in range(groups):
            compact = compact_in[g] + gather_group(tabs, g, sums, lane)
            wide, products = wides.at[g], products_all.at[g]
            channel = lax.broadcasted_iota(jnp.int32, (64, 128), 0) & 3
            mass = jnp.where(channel == 0, compact, 0.0)
            mass = mass + pltpu.roll(mass, 1, 0)
            mass = mass + pltpu.roll(mass, 2, 0)
            node = compact / jnp.maximum(mass, mass_floor)
            node = node - jnp.where(channel == 3, time_step * gravity, 0.0)
            node = jnp.where(inside_ref[g] > 0.5, node, 0.0)
            high, low = split(node)
            both = jnp.concatenate([high, low], axis=1)
            for slot in range(16):
                keep = (lane_row // 8 == slot).astype(BF16)
                keep = jnp.concatenate([keep, keep], axis=1)
                wide[64 * slot : 64 * slot + 64, :] = both * keep
            products[...] = jnp.dot(
                wide[...], depth[g, 0:256, :], preferred_element_type=F32
            ) + jnp.dot(wide[:, 0:128], depth[g, 256:384, :], preferred_element_type=F32)

            def finish(slot, _, g=g, products=products):
                base = (g * 16 + slot) * 16
                weights, moments = y_patterns(params, base, sub)
                x0 = row_of(params, base + 8)
                at = slot * 64
                plain = [None, None]
                along = [None, None]
                deep = [None, None]
                for i in range(4):
                    wx = row_of(params, base + i)
                    wxi = wx * (i - x0)
                    for half in range(2):
                        place = pl.ds(at + 16 * i + 8 * half, 8)
                        one = products[place, 0:128]
                        two = products[place, 128:256]
                        terms = (wx * one, wxi * one, wx * two)
                        for kept, term in zip((plain, along, deep), terms):
                            kept[half] = term if i == 0 else kept[half] + term
                found = (
                    weights[0] * plain[0] + weights[1] * plain[1],
                    weights[0] * along[0] + weights[1] * along[1],
                    moments[0] * plain[0] + moments[1] * plain[1],
                    weights[0] * deep[0] + weights[1] * deep[1],
                )
                place = (g * 16 + slot) * 32
                for kind, value in enumerate(found):
                    results[pl.ds(place + 8 * kind, 8), :] = value + pltpu.roll(value, 4, 0)
                return _

            for slot in range(16):
                finish(slot, 0)

        for g8 in range(bins // 8):
            span = pl.ds(g8 * 8, 8)
            fractions, bases, deform, mass = load8(g8)

            def get(kind, a, g8=g8):
                return results[pl.ds(g8 * 256 + kind * 8 + 1 + a, 8, stride=32), :]

            velocity = [get(0, a) for a in range(3)]
            affine = [4.0 * get(1 + b, a) for a in range(3) for b in range(3)]
            deform = [
                deform[3 * a + b]
                + time_step * sum(affine[3 * a + c] * deform[3 * c + b] for c in range(3))
                for a in range(3)
                for b in range(3)
            ]
            if last:
                for a in range(3):
                    velocity_out[a, span, :] = velocity[a]
                for e in range(9):
                    affine_out[e, span, :] = affine[e]
                    deform_out[e, span, :] = deform[e]
            else:
                fractions = [fractions[a] + time_step * velocity[a] for a in range(3)]
                store8(g8, fractions, bases, deform, mass)
                stencil_rows(g8, fractions, bases, params_out)
                deposit_rows(g8, velocity, affine, deform, mass, blends)

    if not last:
        for g in range(groups):
            depth_weights(g, params_out, depth_out)
            wide, wide_low = wides.at[g], wides_low.at[g]
            products, products_low = products_all.at[g], products_lows.at[g]

            def build(slot, _, g=g, wide=wide, wide_low=wide_low):
                base = (g * 16 + slot) * 16
                place = (g * 16 + slot) * 32
                weights, moments = y_patterns(params_out, base, sub)
                x0 = row_of(params_out, base + 8)
                pushed, b0, b1, b2 = [blends[pl.ds(place + 8 * k, 8), :] for k in range(4)]
                plain = []
                deep = []
                for i in range(4):
                    wx = row_of(params_out, base + i)
                    along = (pushed + b0 * (i - x0)) * wx
                    across = b1 * wx
                    depthwise = b2 * wx
                    for half in range(2):
                        plain.append(along * weights[half] + across * moments[half])
                        deep.append(depthwise * weights[half])
                value = jnp.concatenate([fill(plain), fill(deep)], axis=1)
                high, low = split(value)
                at = pl.ds(slot * 64, 64)
                wide[at, :] = high
                wide_low[at, :] = low
                return _

            for slot in range(16):
                build(slot, 0)
            turned = (((1,), (1,)), ((), ()))
            products[...] = lax.dot_general(
                wide[...], depth_out[g, 128:384, :], turned, preferred_element_type=F32
            )
            products_low[...] = lax.dot_general(
                wide_low[...], depth_out[g, 128:256, :], turned, preferred_element_type=F32
            )
            compact = jnp.zeros((64, 128), F32)
            for slot in range(16):
                at = slice(64 * slot, 64 * slot + 64)
                value = products[at, 0:128] + products[at, 128:256] + products_low[at, :]
                compact = jnp.where(lane // 8 == slot, value, compact)
            patch_out[64 * g : 64 * g + 64, :] = compact


VMEM_SPEC = pl.BlockSpec(memory_space=pltpu.VMEM)
SMEM_SPEC = pl.BlockSpec(memory_space=pltpu.SMEM)


def shape_of(*dims, dtype=F32):
    return jax.ShapeDtypeStruct(dims, dtype)


def grid_rows(total_x):
    return (total_x + 7) * ROWS_X + 16


def limit_for(operands, total_x):
    held = sum(4 * op.size for op in operands) + 512 * grid_rows(total_x)
    return held + (16 << 20)


def run_column(total_x, bins, tabs, column):
    return pl.pallas_call(
        functools.partial(column_kernel, bins),
        out_shape=shape_of(bins // 16, 64, 128),
        in_specs=[SMEM_SPEC, VMEM_SPEC],
        out_specs=VMEM_SPEC,
        scratch_shapes=[pltpu.VMEM((grid_rows(total_x), 128), F32)],
        cost_estimate=pl.CostEstimate(
            flops=column.size * 10, bytes_accessed=column.size * 160, transcendentals=0
        ),
        compiler_params=pltpu.CompilerParams(vmem_limit_bytes=limit_for([column], total_x)),
    )(tabs, column)


def run_kernel(first, listing, last, total_x, bins, operands):
    if last:
        outs = [shape_of(3, bins, 128), shape_of(9, bins, 128), shape_of(9, bins, 128)]
    else:
        outs = [
            shape_of(4 * bins + (8 if first else 0), 128),
            shape_of(16, bins, 128),
            shape_of(16 * bins, 128),
            shape_of(bins // 16, 384, 256, dtype=BF16),
        ]
    out_specs = [VMEM_SPEC] * len(outs)
    scratch = [
        pltpu.VMEM((bins // 16, 1024, 256), BF16),
        pltpu.VMEM((bins // 16, 1024, 256), F32),
    ]
    in_specs = [VMEM_SPEC] * len(operands)
    if first:
        in_specs = [pl.BlockSpec(memory_space=pltpu.HBM)] * len(operands)
        scratch += [pltpu.VMEM(op.shape, op.dtype) for op in operands]
        scratch += [pltpu.SemaphoreType.DMA((len(operands),))]
    else:
        in_specs[0] = SMEM_SPEC
        if listing:
            outs.append(shape_of(2 * operands[1].shape[0] * bins + 8, dtype=jnp.int32))
            out_specs.append(SMEM_SPEC)
        else:
            in_specs[1] = SMEM_SPEC
        scratch += [
            pltpu.VMEM((grid_rows(total_x), 128), F32),
            pltpu.VMEM((32 * bins, 128), F32),
        ]
    if not last:
        scratch += [
            pltpu.VMEM((bins // 16, 1024, 256), BF16),
            pltpu.VMEM((32 * bins, 128), F32),
            pltpu.VMEM((bins // 16, 1024, 128), F32),
        ]
    if first:
        operands = [pltpu.with_memory_space_constraint(op, pltpu.HBM) for op in operands]
    return pl.pallas_call(
        functools.partial(kernel, first, listing, last),
        out_shape=outs,
        in_specs=in_specs,
        out_specs=out_specs,
        scratch_shapes=scratch,
        compiler_params=pltpu.CompilerParams(vmem_limit_bytes=limit_for(operands, total_x)),
    )(*operands)


def column_of(payload):
    count = lax.axis_size("gx")
    if count > 8:
        return lax.all_gather(payload, "gx")
    pieces = [payload]
    for shift in range(1, count):
        pairs = [(i, i ^ shift if count & (count - 1) == 0 else (i + shift) % count) for i in range(count)]
        pieces.append(lax.ppermute(payload, "gx", pairs))
    return jnp.stack(pieces)


def neighbours_of(column):
    count = lax.axis_size("gy")
    got = []
    for start in range(2):
        pairs = []
        for low in range(start, count - 1, 2):
            pairs += [(low, low + 1), (low + 1, low)]
        got.append(lax.ppermute(column, "gy", pairs) if pairs else jnp.zeros_like(column))
    return got


def shards(
    offsets, cell_index, velocity, affine, strain, particle_mass, owner_row, anchor_xy, anchor_z
):
    bins = offsets.shape[0]
    total_x = TILE * lax.axis_size("gx")
    total_y = TILE * lax.axis_size("gy")
    place_y = lax.axis_index("gy")
    turn = lambda array: jnp.transpose(array, (1, 0, 2))
    payload, state, params, depth = run_kernel(
        True,
        False,
        False,
        total_x,
        bins,
        [
            turn(offsets),
            cell_index,
            turn(velocity),
            turn(affine),
            turn(strain),
            particle_mass,
            owner_row.T,
            anchor_xy.T,
            anchor_z[None, :],
        ],
    )
    def inside_grid(late_x, late_y, late_z):
        serial = jnp.arange(64, dtype=jnp.int32)[None, :, None]
        group = bins // 16
        spread = lambda values: jnp.repeat(values.reshape(group, 16), 8, axis=1)[:, None, :]
        at_x = spread(late_x) + serial // 16
        at_y = spread(place_y * TILE + late_y) + serial // 4 % 4
        at_z = spread(late_z) + (jnp.arange(128, dtype=jnp.int32) % 8)[None, None, :]
        channel = serial % 4
        at = jnp.where(channel == 1, at_x, jnp.where(channel == 2, at_y, at_z))
        limit = jnp.where(channel == 1, total_x, jnp.where(channel == 2, total_y, CZ))
        in_grid = (at_x >= 0) & (at_x < total_x) & (at_y >= 0) & (at_y < total_y)
        inside = ((at >= 2) & (at < limit - 2) & (channel > 0) & in_grid).astype(F32)
        return inside

    def places(block, move):
        known = block[:, 4 * bins : 4 * bins + 4, 0:bins].astype(jnp.int32)
        y = known[:, 1] + LOW_Y + move
        row = known[:, 0] * ROWS_X + 4 * y
        good = (known[:, 3] > 0) & (y >= 0) & (y <= LOW_Y + TILE + 1)
        return jnp.where(good, row, -1).reshape(-1), known[:, 2].reshape(-1)

    step_a = jnp.where(place_y % 2 == 0, TILE, -TILE)
    for substep in range(SUBSTEPS):
        column = column_of(payload)
        beside = neighbours_of(column)
        if substep == 0:
            own = payload[4 * bins : 4 * bins + 3, 0:bins].astype(jnp.int32)
            own_row = own[0] * ROWS_X + 4 * (own[1] + LOW_Y)
            anchor_z = own[2]
            late, _ = lax.optimization_barrier((payload[4 * bins : 4 * bins + 3], column))
            late = late[:, 0:bins].astype(jnp.int32)
            inside = inside_grid(late[0] - 2, late[1], late[2])
            row, z = places(column, 0)
            column_tabs = jnp.concatenate([own_row, row, anchor_z, z])
            row_a, z_a = places(beside[0], step_a)
            row_b, z_b = places(beside[1], -step_a)
            tabs = jnp.concatenate([own_row, row_a, row_b, anchor_z, z_a, z_b])
        compact = run_column(total_x, bins, column_tabs, column)
        listing = substep == 0
        last = substep == SUBSTEPS - 1
        results = run_kernel(
            False,
            listing,
            last,
            total_x,
            bins,
            [tabs]
            + ([] if listing else [listed])
            + beside
            + [compact, inside, state, params, depth],
        )
        if not last:
            payload, state, params, depth = results[:4]
        if listing:
            listed = results[4]
    return tuple(turn(array) for array in results)


def solution(mesh):
    wide = P(("runs", "gx", "gy"), None, None)
    flat = P(("runs", "gx", "gy"), None)
    return jax.shard_map(
        shards,
        mesh=mesh,
        in_specs=(wide, flat, wide, wide, wide, flat, flat, flat, P(("runs", "gx", "gy"))),
        out_specs=(wide, wide, wide),
        check_vma=False,
    )
```

```python
import functools

import jax
import jax.numpy as jnp
from jax import lax
from jax.experimental import pallas as pl
from jax.experimental.pallas import tpu as pltpu
from jax.sharding import PartitionSpec as P

TILE = 16
CZ = 128
SUBSTEPS = 4
SPAN_Y = 26
LOW_Y = 5
AT_ONCE = 16
ROWS_X = 4 * SPAN_Y

time_step = 0.05
shear_coef = 2.0
bulk_coef = 2.0
gravity = 2.0
mass_floor = 0.25

F32 = jnp.float32
BF16 = jnp.bfloat16


def split(value):
    high = value.astype(BF16)
    low = (value - high.astype(F32)).astype(BF16)
    return high, low


def quadratic(f):
    lower = 0.5 * (1.5 - f) ** 2
    middle = 0.75 - (f - 1.0) ** 2
    upper = 0.5 * (f - 0.5) ** 2
    return lower, middle, upper


def row_of(ref, at):
    return jnp.broadcast_to(ref[pl.ds(at, 1), :], (8, 128))


def stencil_rows(group, fractions, bases, params):
    def put(row, value):
        params[pl.ds(group * 128 + row, 8, stride=16), :] = value

    for axis in range(2):
        lower, middle, upper = quadratic(fractions[axis])
        first = bases[axis] < 0.5
        put(4 * axis, jnp.where(first, lower, 0.0))
        put(4 * axis + 1, jnp.where(first, middle, lower))
        put(4 * axis + 2, jnp.where(first, upper, middle))
        put(4 * axis + 3, jnp.where(first, 0.0, upper))
        put(8 + axis, bases[axis] + fractions[axis])
    put(10, fractions[2])
    put(11, bases[2])
    for at, value in enumerate(quadratic(fractions[2])):
        put(12 + at, value)


def depth_weights(group, params, depth):
    serial = lax.broadcasted_iota(jnp.int32, (8, 128), 0).astype(F32)

    def one(at):
        base = at * 16
        t = serial - row_of(params, base + 11)
        w = jnp.where(
            t == 0.0,
            row_of(params, base + 12),
            jnp.where(
                t == 1.0,
                row_of(params, base + 13),
                jnp.where(t == 2.0, row_of(params, base + 14), 0.0),
            ),
        )
        return jnp.concatenate([w, (t - row_of(params, base + 10)) * w], axis=1)

    for pair in range(8):
        at = 16 * group + 2 * pair
        high, low = split(jnp.concatenate([one(at), one(at + 1)], axis=0))
        row = 16 * pair
        depth[group, row : row + 16, :] = high
        depth[group, row + 128 : row + 144, :] = high
        depth[group, row + 256 : row + 272, :] = low


def y_patterns(params, base, sub):
    upper_half = sub >= 4
    x1 = row_of(params, base + 9)
    weights = []
    moments = []
    for half in range(2):
        w = jnp.where(
            upper_half, row_of(params, base + 5 + 2 * half), row_of(params, base + 4 + 2 * half)
        )
        j = jnp.where(upper_half, 1.0 + 2 * half, 0.0 + 2 * half)
        weights.append(w)
        moments.append(w * (j - x1))
    return weights, moments


def deposit_rows(group, velocity, affine, deform, mass, blends):
    entries = [[deform[3 * a + b] for b in range(3)] for a in range(3)]
    volume = (
        entries[0][0] * (entries[1][1] * entries[2][2] - entries[1][2] * entries[2][1])
        - entries[0][1] * (entries[1][0] * entries[2][2] - entries[1][2] * entries[2][0])
        + entries[0][2] * (entries[1][0] * entries[2][1] - entries[1][1] * entries[2][0])
    )
    log_volume = jnp.log(volume)

    def put(kind, channel, value):
        for half in range(2):
            blends[pl.ds(group * 256 + kind * 8 + half * 4 + channel, 8, stride=32), :] = value

    zero = jnp.zeros_like(mass)
    put(0, 0, mass)
    for b in range(3):
        put(1 + b, 0, zero)
    for a in range(3):
        put(0, 1 + a, mass * velocity[a])
        for b in range(3):
            product = sum(entries[a][c] * entries[b][c] for c in range(3))
            diagonal = 1.0 if a == b else 0.0
            stress = shear_coef * (product - diagonal) + bulk_coef * log_volume * diagonal
            put(1 + b, 1 + a, mass * affine[3 * a + b] - stress)


def add_patch(sums, row, patch, shift, z, lane):
    moved = pltpu.roll(patch, shift, 1)
    at = lane - z
    inside = (at >= 0) & (at < 8)
    for i in range(4):
        for half in range(2):
            place = pl.ds(row + i * ROWS_X + 8 * half, 8)
            first = 16 * i + 8 * half
            sums[place, :] = sums[place, :] + jnp.where(inside, moved[first : first + 8], 0.0)


def clear_own(tabs, bins, sums):
    for at in range(bins):
        for i in range(4):
            sums[pl.ds(tabs[at] + i * ROWS_X, 16), :] = jnp.zeros((16, 128), F32)


def gather_group(tabs, group, sums, lane):
    total = tabs.shape[0] // 2
    compact = [jnp.zeros((8, 128), F32)] * 8
    for slot in range(16):
        row = tabs[group * 16 + slot]
        z = tabs[total + group * 16 + slot]
        node = fill([sums[pl.ds(row + i * ROWS_X, 16), :] for i in range(4)])
        moved = pltpu.roll(node, (8 * slot + 128 - z) & 127, 1)
        mine = lane // 8 == slot
        compact = [jnp.where(mine, moved[8 * k : 8 * k + 8], compact[k]) for k in range(8)]
    return fill(compact)


def fill(blocks):
    return jnp.concatenate(blocks, axis=0)


def list_bins(tabs, bins, listed, spare):
    total = tabs.shape[0] // 2
    stride = listed.shape[0] // 4

    def one(at, place):
        listed[place] = at
        return place + (tabs[bins + at] >= 0).astype(jnp.int32)

    many = lax.fori_loop(0, total - bins, one, jnp.int32(0), unroll=16)

    def widen(at, _):
        for step in range(AT_ONCE):
            n = at * AT_ONCE + step
            used = n < many
            which = jnp.where(used, listed[n], 0)
            z = tabs[total + bins + which]
            listed[n] = jnp.where(used, tabs[bins + which], spare)
            listed[stride + n] = z
            listed[2 * stride + n] = (z + 128 - 8 * (which & 15)) & 127
            listed[3 * stride + n] = which >> 4
        return _

    lax.fori_loop(0, (many + AT_ONCE - 1) // AT_ONCE, widen, 0)
    listed[stride - 1] = many


def scatter_listed(bins, listed, patch_ref, sums, lane):
    stride = listed.shape[0] // 4
    groups = bins // 16

    def some(at, _):
        found = []
        for step in range(AT_ONCE):
            n = at * AT_ONCE + step
            row, z, shift, block = [listed[k * stride + n] for k in range(4)]
            start = pl.multiple_of((block % groups) * 64, 64)
            found.append((row, patch_ref[block // groups, pl.ds(start, 64), :], shift, z))
        for row, patch, shift, z in found:
            add_patch(sums, row, patch, shift, z, lane)
        return _

    lax.fori_loop(0, (listed[stride - 1] + AT_ONCE - 1) // AT_ONCE, some, 0)


def column_kernel(bins, tabs, patch_ref, out, sums):
    lane = lax.broadcasted_iota(jnp.int32, (8, 128), 1)
    total = tabs.shape[0] // 2
    groups = bins // 16
    clear_own(tabs, bins, sums)

    def block(at, _):
        start = pl.multiple_of((at % groups) * 64, 64)
        first = bins + at * 16
        for slot in range(16):
            z = tabs[total + first + slot]
            patch = patch_ref[at // groups, pl.ds(start, 64), :]
            add_patch(sums, tabs[first + slot], patch, (z + (128 - 8 * slot)) & 127, z, lane)
        return _

    lax.fori_loop(0, patch_ref.shape[0] * groups, block, 0)
    for g in range(groups):
        out[g] = gather_group(tabs, g, sums, lane)


def spare_row(sums):
    return sums.shape[0] - 3 * ROWS_X - 16


def kernel(first, listing, last, *refs):
    refs = list(refs)
    take = lambda n: [refs.pop(0) for _ in range(n)]
    if first:
        sources = take(9)
        bins = sources[5].shape[0]
    else:
        (tabs,) = take(1)
        lists = take(1 if listing else 2)
        sides = take(2)
        compact_in, inside_ref, state_in, params, depth = take(5)
        bins = state_in.shape[1]
    if last:
        velocity_out, affine_out, deform_out = take(3)
    else:
        patch_out, state_out, params_out, depth_out = take(4)
    if listing:
        side_tabs = [tabs] + lists
        lists = take(2)
    wides, products_all = take(2)
    if first:
        held = take(9)
        arrived = refs.pop(0)
        copies = [
            pltpu.make_async_copy(source, target, arrived.at[at])
            for at, (source, target) in enumerate(zip(sources, held))
        ]
        for copy in copies:
            copy.start()
        for copy in copies:
            copy.wait()
        offsets_in, cell, velocity_in, affine_in, strain, mass_in, owner, corner, depth_at = held
        facts = slice(4 * bins, 4 * bins + 8)
        patch_out[facts, :] = jnp.zeros((8, 128), F32)
        known = (owner[...] * TILE + corner[0:1, :] + 2, corner[1:2, :], depth_at[...])
        for at, value in enumerate(known):
            patch_out[4 * bins + at : 4 * bins + at + 1, 0:bins] = value.astype(F32)
        patch_out[4 * bins + 3 : 4 * bins + 4, 0:bins] = jnp.ones((1, bins), F32)
    else:
        sums, results = take(2)
    if not last:
        wides_low, blends, products_lows = take(3)
    groups = bins // 16
    sub = lax.broadcasted_iota(jnp.int32, (8, 128), 0)
    lane = lax.broadcasted_iota(jnp.int32, (8, 128), 1)
    lane_row = lax.broadcasted_iota(jnp.int32, (1, 128), 1)

    def load8(g8):
        span = pl.ds(g8 * 8, 8)
        if first:
            fractions = [offsets_in[a, span, :] for a in range(3)]
            c = cell[span, :]
            bx = (c >= 12).astype(jnp.int32)
            c = c - 12 * bx
            by = (c >= 6).astype(jnp.int32)
            bases = [bx.astype(F32), by.astype(F32), (c - 6 * by).astype(F32)]
            deform = [
                strain[e, span, :] + (1.0 if e % 4 == 0 else 0.0) for e in range(9)
            ]
            return fractions, bases, deform, mass_in[span, :]
        fractions = [state_in[a, span, :] for a in range(3)]
        bases = [state_in[3 + a, span, :] for a in range(3)]
        deform = [state_in[7 + e, span, :] for e in range(9)]
        return fractions, bases, deform, state_in[6, span, :]

    def store8(g8, fractions, bases, deform, mass):
        span = pl.ds(g8 * 8, 8)
        for a in range(3):
            state_out[a, span, :] = fractions[a]
            state_out[3 + a, span, :] = bases[a]
        state_out[6, span, :] = mass
        for e in range(9):
            state_out[7 + e, span, :] = deform[e]

    if first:
        for g8 in range(bins // 8):
            span = pl.ds(g8 * 8, 8)
            fractions, bases, deform, mass = load8(g8)
            store8(g8, fractions, bases, deform, mass)
            stencil_rows(g8, fractions, bases, params_out)
            velocity = [velocity_in[a, span, :] for a in range(3)]
            affine = [affine_in[e, span, :] for e in range(9)]
            deposit_rows(g8, velocity, affine, deform, mass, blends)
    else:
        if listing:
            for own_tabs, listed in zip(side_tabs, lists):
                list_bins(own_tabs, bins, listed, spare_row(sums))
        clear_own(tabs, bins, sums)
        for listed, side_ref in zip(lists, sides):
            scatter_listed(bins, listed, side_ref, sums, lane)
        for g in range(groups):
            compact = compact_in[g] + gather_group(tabs, g, sums, lane)
            wide, products = wides.at[g], products_all.at[g]
            channel = lax.broadcasted_iota(jnp.int32, (64, 128), 0) & 3
            mass = jnp.where(channel == 0, compact, 0.0)
            mass = mass + pltpu.roll(mass, 1, 0)
            mass = mass + pltpu.roll(mass, 2, 0)
            node = compact / jnp.maximum(mass, mass_floor)
            node = node - jnp.where(channel == 3, time_step * gravity, 0.0)
            node = jnp.where(inside_ref[g] > 0.5, node, 0.0)
            high, low = split(node)
            both = jnp.concatenate([high, low], axis=1)
            for slot in range(16):
                keep = (lane_row // 8 == slot).astype(BF16)
                keep = jnp.concatenate([keep, keep], axis=1)
                wide[64 * slot : 64 * slot + 64, :] = both * keep
            products[...] = jnp.dot(
                wide[...], depth[g, 0:256, :], preferred_element_type=F32
            ) + jnp.dot(wide[:, 0:128], depth[g, 256:384, :], preferred_element_type=F32)

            def finish(slot, _, g=g, products=products):
                base = (g * 16 + slot) * 16
                weights, moments = y_patterns(params, base, sub)
                x0 = row_of(params, base + 8)
                at = slot * 64
                plain = [None, None]
                along = [None, None]
                deep = [None, None]
                for i in range(4):
                    wx = row_of(params, base + i)
                    wxi = wx * (i - x0)
                    for half in range(2):
                        place = pl.ds(at + 16 * i + 8 * half, 8)
                        one = products[place, 0:128]
                        two = products[place, 128:256]
                        terms = (wx * one, wxi * one, wx * two)
                        for kept, term in zip((plain, along, deep), terms):
                            kept[half] = term if i == 0 else kept[half] + term
                found = (
                    weights[0] * plain[0] + weights[1] * plain[1],
                    weights[0] * along[0] + weights[1] * along[1],
                    moments[0] * plain[0] + moments[1] * plain[1],
                    weights[0] * deep[0] + weights[1] * deep[1],
                )
                place = (g * 16 + slot) * 32
                for kind, value in enumerate(found):
                    results[pl.ds(place + 8 * kind, 8), :] = value + pltpu.roll(value, 4, 0)
                return _

            for slot in range(16):
                finish(slot, 0)

        for g8 in range(bins // 8):
            span = pl.ds(g8 * 8, 8)
            fractions, bases, deform, mass = load8(g8)

            def get(kind, a, g8=g8):
                return results[pl.ds(g8 * 256 + kind * 8 + 1 + a, 8, stride=32), :]

            velocity = [get(0, a) for a in range(3)]
            affine = [4.0 * get(1 + b, a) for a in range(3) for b in range(3)]
            deform = [
                deform[3 * a + b]
                + time_step * sum(affine[3 * a + c] * deform[3 * c + b] for c in range(3))
                for a in range(3)
                for b in range(3)
            ]
            if last:
                for a in range(3):
                    velocity_out[a, span, :] = velocity[a]
                for e in range(9):
                    affine_out[e, span, :] = affine[e]
                    deform_out[e, span, :] = deform[e]
            else:
                fractions = [fractions[a] + time_step * velocity[a] for a in range(3)]
                store8(g8, fractions, bases, deform, mass)
                stencil_rows(g8, fractions, bases, params_out)
                deposit_rows(g8, velocity, affine, deform, mass, blends)

    if not last:
        for g in range(groups):
            depth_weights(g, params_out, depth_out)
            wide, wide_low = wides.at[g], wides_low.at[g]
            products, products_low = products_all.at[g], products_lows.at[g]

            def build(slot, _, g=g, wide=wide, wide_low=wide_low):
                base = (g * 16 + slot) * 16
                place = (g * 16 + slot) * 32
                weights, moments = y_patterns(params_out, base, sub)
                x0 = row_of(params_out, base + 8)
                pushed, b0, b1, b2 = [blends[pl.ds(place + 8 * k, 8), :] for k in range(4)]
                plain = []
                deep = []
                for i in range(4):
                    wx = row_of(params_out, base + i)
                    along = (pushed + b0 * (i - x0)) * wx
                    across = b1 * wx
                    depthwise = b2 * wx
                    for half in range(2):
                        plain.append(along * weights[half] + across * moments[half])
                        deep.append(depthwise * weights[half])
                value = jnp.concatenate([fill(plain), fill(deep)], axis=1)
                high, low = split(value)
                at = pl.ds(slot * 64, 64)
                wide[at, :] = high
                wide_low[at, :] = low
                return _

            for slot in range(16):
                build(slot, 0)
            turned = (((1,), (1,)), ((), ()))
            products[...] = lax.dot_general(
                wide[...], depth_out[g, 128:384, :], turned, preferred_element_type=F32
            )
            products_low[...] = lax.dot_general(
                wide_low[...], depth_out[g, 128:256, :], turned, preferred_element_type=F32
            )
            compact = [jnp.zeros((8, 128), F32)] * 8
            for slot in range(16):
                mine = lane // 8 == slot
                for k in range(8):
                    at = slice(64 * slot + 8 * k, 64 * slot + 8 * k + 8)
                    value = products[at, 0:128] + products[at, 128:256] + products_low[at, :]
                    compact[k] = jnp.where(mine, value, compact[k])
            patch_out[64 * g : 64 * g + 64, :] = fill(compact)


VMEM_SPEC = pl.BlockSpec(memory_space=pltpu.VMEM)
SMEM_SPEC = pl.BlockSpec(memory_space=pltpu.SMEM)


def shape_of(*dims, dtype=F32):
    return jax.ShapeDtypeStruct(dims, dtype)


def grid_rows(total_x):
    return (total_x + 7) * ROWS_X + 16


def limit_for(operands, total_x):
    held = sum(4 * op.size for op in operands) + 512 * grid_rows(total_x)
    return held + (16 << 20)


def list_shape(bins_near):
    stride = bins_near + AT_ONCE + 8
    return shape_of(4 * stride, dtype=jnp.int32)


def run_column(total_x, bins, tabs, column):
    return pl.pallas_call(
        functools.partial(column_kernel, bins),
        out_shape=shape_of(bins // 16, 64, 128),
        in_specs=[SMEM_SPEC, VMEM_SPEC],
        out_specs=VMEM_SPEC,
        scratch_shapes=[pltpu.VMEM((grid_rows(total_x), 128), F32)],
        cost_estimate=pl.CostEstimate(
            flops=column.size * 10, bytes_accessed=column.size * 160, transcendentals=0
        ),
        compiler_params=pltpu.CompilerParams(vmem_limit_bytes=limit_for([column], total_x)),
    )(tabs, column)


def run_kernel(first, listing, last, total_x, bins, operands):
    if last:
        outs = [shape_of(3, bins, 128), shape_of(9, bins, 128), shape_of(9, bins, 128)]
    else:
        outs = [
            shape_of(4 * bins + (8 if first else 0), 128),
            shape_of(16, bins, 128),
            shape_of(16 * bins, 128),
            shape_of(bins // 16, 384, 256, dtype=BF16),
        ]
    out_specs = [VMEM_SPEC] * len(outs)
    scratch = [
        pltpu.VMEM((bins // 16, 1024, 256), BF16),
        pltpu.VMEM((bins // 16, 1024, 256), F32),
    ]
    in_specs = [VMEM_SPEC] * len(operands)
    if first:
        in_specs = [pl.BlockSpec(memory_space=pltpu.HBM)] * len(operands)
        scratch += [pltpu.VMEM(op.shape, op.dtype) for op in operands]
        scratch += [pltpu.SemaphoreType.DMA((len(operands),))]
    else:
        scalars = 2 if listing else 3
        in_specs[:scalars] = [SMEM_SPEC] * scalars
        if listing:
            outs += [list_shape(operands[scalars].shape[0] * bins)] * 2
            out_specs += [SMEM_SPEC] * 2
        scratch += [
            pltpu.VMEM((grid_rows(total_x), 128), F32),
            pltpu.VMEM((32 * bins, 128), F32),
        ]
    if not last:
        scratch += [
            pltpu.VMEM((bins // 16, 1024, 256), BF16),
            pltpu.VMEM((32 * bins, 128), F32),
            pltpu.VMEM((bins // 16, 1024, 128), F32),
        ]
    if first:
        operands = [pltpu.with_memory_space_constraint(op, pltpu.HBM) for op in operands]
    return pl.pallas_call(
        functools.partial(kernel, first, listing, last),
        out_shape=outs,
        in_specs=in_specs,
        out_specs=out_specs,
        scratch_shapes=scratch,
        compiler_params=pltpu.CompilerParams(vmem_limit_bytes=limit_for(operands, total_x)),
    )(*operands)


def column_of(payload):
    count = lax.axis_size("gx")
    if count > 8:
        return lax.all_gather(payload, "gx")
    pieces = [payload]
    for shift in range(1, count):
        pairs = [(i, i ^ shift if count & (count - 1) == 0 else (i + shift) % count) for i in range(count)]
        pieces.append(lax.ppermute(payload, "gx", pairs))
    return jnp.stack(pieces)


def neighbour_of(column, start):
    count = lax.axis_size("gy")
    pairs = []
    for low in range(start, count - 1, 2):
        pairs += [(low, low + 1), (low + 1, low)]
    return lax.ppermute(column, "gy", pairs) if pairs else jnp.zeros_like(column)


def shards(
    offsets, cell_index, velocity, affine, strain, particle_mass, owner_row, anchor_xy, anchor_z
):
    bins = offsets.shape[0]
    total_x = TILE * lax.axis_size("gx")
    total_y = TILE * lax.axis_size("gy")
    place_y = lax.axis_index("gy")
    turn = lambda array: jnp.transpose(array, (1, 0, 2))
    payload, state, params, depth = run_kernel(
        True,
        False,
        False,
        total_x,
        bins,
        [
            turn(offsets),
            cell_index,
            turn(velocity),
            turn(affine),
            turn(strain),
            particle_mass,
            owner_row.T,
            anchor_xy.T,
            anchor_z[None, :],
        ],
    )
    def inside_grid(late_x, late_y, late_z):
        serial = jnp.arange(64, dtype=jnp.int32)[None, :, None]
        group = bins // 16
        spread = lambda values: jnp.repeat(values.reshape(group, 16), 8, axis=1)[:, None, :]
        at_x = spread(late_x) + serial // 16
        at_y = spread(place_y * TILE + late_y) + serial // 4 % 4
        at_z = spread(late_z) + (jnp.arange(128, dtype=jnp.int32) % 8)[None, None, :]
        channel = serial % 4
        at = jnp.where(channel == 1, at_x, jnp.where(channel == 2, at_y, at_z))
        limit = jnp.where(channel == 1, total_x, jnp.where(channel == 2, total_y, CZ))
        in_grid = (at_x >= 0) & (at_x < total_x) & (at_y >= 0) & (at_y < total_y)
        inside = ((at >= 2) & (at < limit - 2) & (channel > 0) & in_grid).astype(F32)
        return inside

    def places(block, move):
        known = block[:, 0:4, 0:bins].astype(jnp.int32)
        y = known[:, 1] + LOW_Y + move
        row = known[:, 0] * ROWS_X + 4 * y
        good = (known[:, 3] > 0) & (y >= 0) & (y <= LOW_Y + TILE + 1)
        return jnp.where(good, row, -1).reshape(-1), known[:, 2].reshape(-1)

    step_a = jnp.where(place_y % 2 == 0, TILE, -TILE)
    for substep in range(SUBSTEPS):
        column = column_of(payload)
        beside_a, beside_b = neighbour_of(column, 0), neighbour_of(column, 1)
        if substep == 0:
            own = payload[4 * bins : 4 * bins + 3, 0:bins].astype(jnp.int32)
            own_row = own[0] * ROWS_X + 4 * (own[1] + LOW_Y)
            anchor_z = own[2]
            late, _ = lax.optimization_barrier((payload[4 * bins : 4 * bins + 3], column))
            late = late[:, 0:bins].astype(jnp.int32)
            inside = inside_grid(late[0] - 2, late[1], late[2])
            row, z = places(column[:, 4 * bins :], 0)
            column_tabs = jnp.concatenate([own_row, row, anchor_z, z])
        compact = run_column(total_x, bins, column_tabs, column)
        listing = substep == 0
        if listing:
            facts_a, facts_b, _ = lax.optimization_barrier(
                (beside_a[:, 4 * bins :], beside_b[:, 4 * bins :], compact)
            )
            row_a, z_a = places(facts_a, step_a)
            row_b, z_b = places(facts_b, -step_a)
            tabs_a = jnp.concatenate([own_row, row_a, anchor_z, z_a])
            tabs_b = jnp.concatenate([own_row, row_b, anchor_z, z_b])
        last = substep == SUBSTEPS - 1
        results = run_kernel(
            False,
            listing,
            last,
            total_x,
            bins,
            [tabs_a] + ([tabs_b] if listing else [list_a, list_b])
            + [beside_a, beside_b, compact, inside, state, params, depth],
        )
        if not last:
            payload, state, params, depth = results[:4]
        if listing:
            list_a, list_b = results[4:]
    return tuple(turn(array) for array in results)


def solution(mesh):
    wide = P(("runs", "gx", "gy"), None, None)
    flat = P(("runs", "gx", "gy"), None)
    return jax.shard_map(
        shards,
        mesh=mesh,
        in_specs=(wide, flat, wide, wide, wide, flat, flat, flat, P(("runs", "gx", "gy"))),
        out_specs=(wide, wide, wide),
        check_vma=False,
    )
```

```python
import functools

import jax
import jax.numpy as jnp
from jax import lax
from jax.experimental import pallas as pl
from jax.experimental.pallas import tpu as pltpu
from jax.sharding import PartitionSpec as P

TILE = 16
CZ = 128
SUBSTEPS = 4
SPAN_Y = 26
LOW_Y = 5
AT_ONCE = 8
ROWS_X = 4 * SPAN_Y

time_step = 0.05
shear_coef = 2.0
bulk_coef = 2.0
gravity = 2.0
mass_floor = 0.25

F32 = jnp.float32
BF16 = jnp.bfloat16


def split(value):
    high = value.astype(BF16)
    low = (value - high.astype(F32)).astype(BF16)
    return high, low


def quadratic(f):
    lower = 0.5 * (1.5 - f) ** 2
    middle = 0.75 - (f - 1.0) ** 2
    upper = 0.5 * (f - 0.5) ** 2
    return lower, middle, upper


def row_of(ref, at):
    return jnp.broadcast_to(ref[pl.ds(at, 1), :], (8, 128))


def stencil_rows(group, fractions, bases, params):
    def put(row, value):
        params[pl.ds(group * 128 + row, 8, stride=16), :] = value

    for axis in range(2):
        lower, middle, upper = quadratic(fractions[axis])
        first = bases[axis] < 0.5
        put(4 * axis, jnp.where(first, lower, 0.0))
        put(4 * axis + 1, jnp.where(first, middle, lower))
        put(4 * axis + 2, jnp.where(first, upper, middle))
        put(4 * axis + 3, jnp.where(first, 0.0, upper))
        put(8 + axis, bases[axis] + fractions[axis])
    put(10, fractions[2])
    put(11, bases[2])
    for at, value in enumerate(quadratic(fractions[2])):
        put(12 + at, value)


def depth_weights(group, params, depth):
    serial = lax.broadcasted_iota(jnp.int32, (8, 128), 0).astype(F32)

    def one(at):
        base = at * 16
        t = serial - row_of(params, base + 11)
        w = jnp.where(
            t == 0.0,
            row_of(params, base + 12),
            jnp.where(
                t == 1.0,
                row_of(params, base + 13),
                jnp.where(t == 2.0, row_of(params, base + 14), 0.0),
            ),
        )
        return jnp.concatenate([w, (t - row_of(params, base + 10)) * w], axis=1)

    for pair in range(8):
        at = 16 * group + 2 * pair
        high, low = split(jnp.concatenate([one(at), one(at + 1)], axis=0))
        row = 16 * pair
        depth[group, row : row + 16, :] = high
        depth[group, row + 128 : row + 144, :] = high
        depth[group, row + 256 : row + 272, :] = low


def y_patterns(params, base, sub):
    upper_half = sub >= 4
    x1 = row_of(params, base + 9)
    weights = []
    moments = []
    for half in range(2):
        w = jnp.where(
            upper_half, row_of(params, base + 5 + 2 * half), row_of(params, base + 4 + 2 * half)
        )
        j = jnp.where(upper_half, 1.0 + 2 * half, 0.0 + 2 * half)
        weights.append(w)
        moments.append(w * (j - x1))
    return weights, moments


def deposit_rows(group, velocity, affine, deform, mass, blends):
    entries = [[deform[3 * a + b] for b in range(3)] for a in range(3)]
    volume = (
        entries[0][0] * (entries[1][1] * entries[2][2] - entries[1][2] * entries[2][1])
        - entries[0][1] * (entries[1][0] * entries[2][2] - entries[1][2] * entries[2][0])
        + entries[0][2] * (entries[1][0] * entries[2][1] - entries[1][1] * entries[2][0])
    )
    log_volume = jnp.log(volume)

    def put(kind, channel, value):
        for half in range(2):
            blends[pl.ds(group * 256 + kind * 8 + half * 4 + channel, 8, stride=32), :] = value

    zero = jnp.zeros_like(mass)
    put(0, 0, mass)
    for b in range(3):
        put(1 + b, 0, zero)
    for a in range(3):
        put(0, 1 + a, mass * velocity[a])
        for b in range(3):
            product = sum(entries[a][c] * entries[b][c] for c in range(3))
            diagonal = 1.0 if a == b else 0.0
            stress = shear_coef * (product - diagonal) + bulk_coef * log_volume * diagonal
            put(1 + b, 1 + a, mass * affine[3 * a + b] - stress)


def add_patch(sums, row, patch, shift, z, lane):
    moved = pltpu.roll(patch, shift, 1)
    at = lane - z
    inside = (at >= 0) & (at < 8)
    for i in range(4):
        for half in range(2):
            place = pl.ds(row + i * ROWS_X + 8 * half, 8)
            first = 16 * i + 8 * half
            sums[place, :] = sums[place, :] + jnp.where(inside, moved[first : first + 8], 0.0)


def clear_own(tabs, bins, sums):
    for at in range(bins):
        for i in range(4):
            sums[pl.ds(tabs[at] + i * ROWS_X, 16), :] = jnp.zeros((16, 128), F32)


def gather_group(tabs, group, sums, lane):
    total = tabs.shape[0] // 2
    compact = [jnp.zeros((8, 128), F32)] * 8
    for slot in range(16):
        row = tabs[group * 16 + slot]
        z = tabs[total + group * 16 + slot]
        node = fill([sums[pl.ds(row + i * ROWS_X, 16), :] for i in range(4)])
        moved = pltpu.roll(node, (8 * slot + 128 - z) & 127, 1)
        mine = lane // 8 == slot
        compact = [jnp.where(mine, moved[8 * k : 8 * k + 8], compact[k]) for k in range(8)]
    return fill(compact)


def fill(blocks):
    return jnp.concatenate(blocks, axis=0)


def list_bins(tabs, bins, listed, spare):
    total = tabs.shape[0] // 2
    stride = listed.shape[0] // 4

    def one(at, place):
        listed[place] = at
        return place + (tabs[bins + at] >= 0).astype(jnp.int32)

    many = lax.fori_loop(0, total - bins, one, jnp.int32(0), unroll=16)

    def widen(at, _):
        for step in range(AT_ONCE):
            n = at * AT_ONCE + step
            used = n < many
            which = jnp.where(used, listed[n], 0)
            z = tabs[total + bins + which]
            listed[n] = jnp.where(used, tabs[bins + which], spare)
            listed[stride + n] = z
            listed[2 * stride + n] = (z + 128 - 8 * (which & 15)) & 127
            listed[3 * stride + n] = which >> 4
        return _

    lax.fori_loop(0, (many + AT_ONCE - 1) // AT_ONCE, widen, 0)
    listed[stride - 1] = many


def scatter_listed(bins, listed, patch_ref, sums, lane):
    stride = listed.shape[0] // 4
    groups = bins // 16

    def some(at, _):
        found = []
        for step in range(AT_ONCE):
            n = at * AT_ONCE + step
            row, z, shift, block = [listed[k * stride + n] for k in range(4)]
            start = pl.multiple_of((block % groups) * 64, 64)
            found.append((row, patch_ref[block // groups, pl.ds(start, 64), :], shift, z))
        for row, patch, shift, z in found:
            add_patch(sums, row, patch, shift, z, lane)
        return _

    lax.fori_loop(0, (listed[stride - 1] + AT_ONCE - 1) // AT_ONCE, some, 0)


def column_kernel(bins, tabs, patch_ref, out, sums):
    lane = lax.broadcasted_iota(jnp.int32, (8, 128), 1)
    total = tabs.shape[0] // 2
    groups = bins // 16
    clear_own(tabs, bins, sums)

    def block(at, _):
        start = pl.multiple_of((at % groups) * 64, 64)
        first = bins + at * 16
        for slot in range(16):
            z = tabs[total + first + slot]
            patch = patch_ref[at // groups, pl.ds(start, 64), :]
            add_patch(sums, tabs[first + slot], patch, (z + (128 - 8 * slot)) & 127, z, lane)
        return _

    lax.fori_loop(0, patch_ref.shape[0] * groups, block, 0)
    for g in range(groups):
        out[g] = gather_group(tabs, g, sums, lane)


def spare_row(sums):
    return sums.shape[0] - 3 * ROWS_X - 16


def kernel(first, listing, last, *refs):
    refs = list(refs)
    take = lambda n: [refs.pop(0) for _ in range(n)]
    if first:
        sources = take(9)
        bins = sources[5].shape[0]
    else:
        (tabs,) = take(1)
        lists = take(1 if listing else 2)
        sides = take(2)
        compact_in, inside_ref, state_in, params, depth = take(5)
        bins = state_in.shape[1]
    if last:
        velocity_out, affine_out, deform_out = take(3)
    else:
        patch_out, state_out, params_out, depth_out = take(4)
    if listing:
        side_tabs = [tabs] + lists
        lists = take(2)
    wides, products_all = take(2)
    if first:
        held = take(9)
        arrived = refs.pop(0)
        copies = [
            pltpu.make_async_copy(source, target, arrived.at[at])
            for at, (source, target) in enumerate(zip(sources, held))
        ]
        for copy in copies:
            copy.start()
        for copy in copies:
            copy.wait()
        offsets_in, cell, velocity_in, affine_in, strain, mass_in, owner, corner, depth_at = held
        facts = slice(4 * bins, 4 * bins + 8)
        patch_out[facts, :] = jnp.zeros((8, 128), F32)
        known = (owner[...] * TILE + corner[0:1, :] + 2, corner[1:2, :], depth_at[...])
        for at, value in enumerate(known):
            patch_out[4 * bins + at : 4 * bins + at + 1, 0:bins] = value.astype(F32)
        patch_out[4 * bins + 3 : 4 * bins + 4, 0:bins] = jnp.ones((1, bins), F32)
    else:
        sums, results = take(2)
    if not last:
        wides_low, blends, products_lows = take(3)
    groups = bins // 16
    sub = lax.broadcasted_iota(jnp.int32, (8, 128), 0)
    lane = lax.broadcasted_iota(jnp.int32, (8, 128), 1)
    lane_row = lax.broadcasted_iota(jnp.int32, (1, 128), 1)

    def load8(g8):
        span = pl.ds(g8 * 8, 8)
        if first:
            fractions = [offsets_in[a, span, :] for a in range(3)]
            c = cell[span, :]
            bx = (c >= 12).astype(jnp.int32)
            c = c - 12 * bx
            by = (c >= 6).astype(jnp.int32)
            bases = [bx.astype(F32), by.astype(F32), (c - 6 * by).astype(F32)]
            deform = [
                strain[e, span, :] + (1.0 if e % 4 == 0 else 0.0) for e in range(9)
            ]
            return fractions, bases, deform, mass_in[span, :]
        fractions = [state_in[a, span, :] for a in range(3)]
        bases = [state_in[3 + a, span, :] for a in range(3)]
        deform = [state_in[7 + e, span, :] for e in range(9)]
        return fractions, bases, deform, state_in[6, span, :]

    def store8(g8, fractions, bases, deform, mass):
        span = pl.ds(g8 * 8, 8)
        for a in range(3):
            state_out[a, span, :] = fractions[a]
            state_out[3 + a, span, :] = bases[a]
        state_out[6, span, :] = mass
        for e in range(9):
            state_out[7 + e, span, :] = deform[e]

    if first:
        for g8 in range(bins // 8):
            span = pl.ds(g8 * 8, 8)
            fractions, bases, deform, mass = load8(g8)
            store8(g8, fractions, bases, deform, mass)
            stencil_rows(g8, fractions, bases, params_out)
            velocity = [velocity_in[a, span, :] for a in range(3)]
            affine = [affine_in[e, span, :] for e in range(9)]
            deposit_rows(g8, velocity, affine, deform, mass, blends)
    else:
        if listing:
            for own_tabs, listed in zip(side_tabs, lists):
                list_bins(own_tabs, bins, listed, spare_row(sums))
        clear_own(tabs, bins, sums)
        for listed, side_ref in zip(lists, sides):
            scatter_listed(bins, listed, side_ref, sums, lane)
        for g in range(groups):
            compact = compact_in[g] + gather_group(tabs, g, sums, lane)
            wide, products = wides.at[g], products_all.at[g]
            channel = lax.broadcasted_iota(jnp.int32, (64, 128), 0) & 3
            mass = jnp.where(channel == 0, compact, 0.0)
            mass = mass + pltpu.roll(mass, 1, 0)
            mass = mass + pltpu.roll(mass, 2, 0)
            node = compact / jnp.maximum(mass, mass_floor)
            node = node - jnp.where(channel == 3, time_step * gravity, 0.0)
            node = jnp.where(inside_ref[g] > 0.5, node, 0.0)
            high, low = split(node)
            both = jnp.concatenate([high, low], axis=1)
            for slot in range(16):
                keep = (lane_row // 8 == slot).astype(BF16)
                keep = jnp.concatenate([keep, keep], axis=1)
                wide[64 * slot : 64 * slot + 64, :] = both * keep
            products[...] = jnp.dot(
                wide[...], depth[g, 0:256, :], preferred_element_type=F32
            ) + jnp.dot(wide[:, 0:128], depth[g, 256:384, :], preferred_element_type=F32)

            def finish(slot, _, g=g, products=products):
                base = (g * 16 + slot) * 16
                weights, moments = y_patterns(params, base, sub)
                x0 = row_of(params, base + 8)
                at = slot * 64
                plain = [None, None]
                along = [None, None]
                deep = [None, None]
                for i in range(4):
                    wx = row_of(params, base + i)
                    wxi = wx * (i - x0)
                    for half in range(2):
                        place = pl.ds(at + 16 * i + 8 * half, 8)
                        one = products[place, 0:128]
                        two = products[place, 128:256]
                        terms = (wx * one, wxi * one, wx * two)
                        for kept, term in zip((plain, along, deep), terms):
                            kept[half] = term if i == 0 else kept[half] + term
                found = (
                    weights[0] * plain[0] + weights[1] * plain[1],
                    weights[0] * along[0] + weights[1] * along[1],
                    moments[0] * plain[0] + moments[1] * plain[1],
                    weights[0] * deep[0] + weights[1] * deep[1],
                )
                place = (g * 16 + slot) * 32
                for kind, value in enumerate(found):
                    results[pl.ds(place + 8 * kind, 8), :] = value + pltpu.roll(value, 4, 0)
                return _

            for slot in range(16):
                finish(slot, 0)

        for g8 in range(bins // 8):
            span = pl.ds(g8 * 8, 8)
            fractions, bases, deform, mass = load8(g8)

            def get(kind, a, g8=g8):
                return results[pl.ds(g8 * 256 + kind * 8 + 1 + a, 8, stride=32), :]

            velocity = [get(0, a) for a in range(3)]
            affine = [4.0 * get(1 + b, a) for a in range(3) for b in range(3)]
            deform = [
                deform[3 * a + b]
                + time_step * sum(affine[3 * a + c] * deform[3 * c + b] for c in range(3))
                for a in range(3)
                for b in range(3)
            ]
            if last:
                for a in range(3):
                    velocity_out[a, span, :] = velocity[a]
                for e in range(9):
                    affine_out[e, span, :] = affine[e]
                    deform_out[e, span, :] = deform[e]
            else:
                fractions = [fractions[a] + time_step * velocity[a] for a in range(3)]
                store8(g8, fractions, bases, deform, mass)
                stencil_rows(g8, fractions, bases, params_out)
                deposit_rows(g8, velocity, affine, deform, mass, blends)

    if not last:
        for g in range(groups):
            depth_weights(g, params_out, depth_out)
            wide, wide_low = wides.at[g], wides_low.at[g]
            products, products_low = products_all.at[g], products_lows.at[g]

            def build(slot, _, g=g, wide=wide, wide_low=wide_low):
                base = (g * 16 + slot) * 16
                place = (g * 16 + slot) * 32
                weights, moments = y_patterns(params_out, base, sub)
                x0 = row_of(params_out, base + 8)
                pushed, b0, b1, b2 = [blends[pl.ds(place + 8 * k, 8), :] for k in range(4)]
                plain = []
                deep = []
                for i in range(4):
                    wx = row_of(params_out, base + i)
                    along = (pushed + b0 * (i - x0)) * wx
                    across = b1 * wx
                    depthwise = b2 * wx
                    for half in range(2):
                        plain.append(along * weights[half] + across * moments[half])
                        deep.append(depthwise * weights[half])
                value = jnp.concatenate([fill(plain), fill(deep)], axis=1)
                high, low = split(value)
                at = pl.ds(slot * 64, 64)
                wide[at, :] = high
                wide_low[at, :] = low
                return _

            for slot in range(16):
                build(slot, 0)
            turned = (((1,), (1,)), ((), ()))
            products[...] = lax.dot_general(
                wide[...], depth_out[g, 128:384, :], turned, preferred_element_type=F32
            )
            products_low[...] = lax.dot_general(
                wide_low[...], depth_out[g, 128:256, :], turned, preferred_element_type=F32
            )
            compact = [jnp.zeros((8, 128), F32)] * 8
            for slot in range(16):
                mine = lane // 8 == slot
                for k in range(8):
                    at = slice(64 * slot + 8 * k, 64 * slot + 8 * k + 8)
                    value = products[at, 0:128] + products[at, 128:256] + products_low[at, :]
                    compact[k] = jnp.where(mine, value, compact[k])
            patch_out[64 * g : 64 * g + 64, :] = fill(compact)


VMEM_SPEC = pl.BlockSpec(memory_space=pltpu.VMEM)
SMEM_SPEC = pl.BlockSpec(memory_space=pltpu.SMEM)


def shape_of(*dims, dtype=F32):
    return jax.ShapeDtypeStruct(dims, dtype)


def grid_rows(total_x):
    return (total_x + 7) * ROWS_X + 16


def limit_for(operands, total_x):
    held = sum(4 * op.size for op in operands) + 512 * grid_rows(total_x)
    return held + (16 << 20)


def list_shape(bins_near):
    stride = bins_near + AT_ONCE + 8
    return shape_of(4 * stride, dtype=jnp.int32)


def run_column(total_x, bins, tabs, column):
    return pl.pallas_call(
        functools.partial(column_kernel, bins),
        out_shape=shape_of(bins // 16, 64, 128),
        in_specs=[SMEM_SPEC, VMEM_SPEC],
        out_specs=VMEM_SPEC,
        scratch_shapes=[pltpu.VMEM((grid_rows(total_x), 128), F32)],
        cost_estimate=pl.CostEstimate(
            flops=column.size * 10, bytes_accessed=column.size * 160, transcendentals=0
        ),
        compiler_params=pltpu.CompilerParams(vmem_limit_bytes=limit_for([column], total_x)),
    )(tabs, column)


def run_kernel(first, listing, last, total_x, bins, operands):
    if last:
        outs = [shape_of(3, bins, 128), shape_of(9, bins, 128), shape_of(9, bins, 128)]
    else:
        outs = [
            shape_of(4 * bins + (8 if first else 0), 128),
            shape_of(16, bins, 128),
            shape_of(16 * bins, 128),
            shape_of(bins // 16, 384, 256, dtype=BF16),
        ]
    out_specs = [VMEM_SPEC] * len(outs)
    scratch = [
        pltpu.VMEM((bins // 16, 1024, 256), BF16),
        pltpu.VMEM((bins // 16, 1024, 256), F32),
    ]
    in_specs = [VMEM_SPEC] * len(operands)
    if first:
        in_specs = [pl.BlockSpec(memory_space=pltpu.HBM)] * len(operands)
        scratch += [pltpu.VMEM(op.shape, op.dtype) for op in operands]
        scratch += [pltpu.SemaphoreType.DMA((len(operands),))]
    else:
        scalars = 2 if listing else 3
        in_specs[:scalars] = [SMEM_SPEC] * scalars
        if listing:
            outs += [list_shape(operands[scalars].shape[0] * bins)] * 2
            out_specs += [SMEM_SPEC] * 2
        scratch += [
            pltpu.VMEM((grid_rows(total_x), 128), F32),
            pltpu.VMEM((32 * bins, 128), F32),
        ]
    if not last:
        scratch += [
            pltpu.VMEM((bins // 16, 1024, 256), BF16),
            pltpu.VMEM((32 * bins, 128), F32),
            pltpu.VMEM((bins // 16, 1024, 128), F32),
        ]
    if first:
        operands = [pltpu.with_memory_space_constraint(op, pltpu.HBM) for op in operands]
    return pl.pallas_call(
        functools.partial(kernel, first, listing, last),
        out_shape=outs,
        in_specs=in_specs,
        out_specs=out_specs,
        scratch_shapes=scratch,
        compiler_params=pltpu.CompilerParams(vmem_limit_bytes=limit_for(operands, total_x)),
    )(*operands)


def column_of(payload):
    count = lax.axis_size("gx")
    if count > 8:
        return lax.all_gather(payload, "gx")
    pieces = [payload]
    for shift in range(1, count):
        pairs = [(i, i ^ shift if count & (count - 1) == 0 else (i + shift) % count) for i in range(count)]
        pieces.append(lax.ppermute(payload, "gx", pairs))
    return jnp.stack(pieces)


def neighbour_of(column, start):
    count = lax.axis_size("gy")
    pairs = []
    for low in range(start, count - 1, 2):
        pairs += [(low, low + 1), (low + 1, low)]
    return lax.ppermute(column, "gy", pairs) if pairs else jnp.zeros_like(column)


def shards(
    offsets, cell_index, velocity, affine, strain, particle_mass, owner_row, anchor_xy, anchor_z
):
    bins = offsets.shape[0]
    total_x = TILE * lax.axis_size("gx")
    total_y = TILE * lax.axis_size("gy")
    place_y = lax.axis_index("gy")
    turn = lambda array: jnp.transpose(array, (1, 0, 2))
    payload, state, params, depth = run_kernel(
        True,
        False,
        False,
        total_x,
        bins,
        [
            turn(offsets),
            cell_index,
            turn(velocity),
            turn(affine),
            turn(strain),
            particle_mass,
            owner_row.T,
            anchor_xy.T,
            anchor_z[None, :],
        ],
    )
    def inside_grid(late_x, late_y, late_z):
        serial = jnp.arange(64, dtype=jnp.int32)[None, :, None]
        group = bins // 16
        spread = lambda values: jnp.repeat(values.reshape(group, 16), 8, axis=1)[:, None, :]
        at_x = spread(late_x) + serial // 16
        at_y = spread(place_y * TILE + late_y) + serial // 4 % 4
        at_z = spread(late_z) + (jnp.arange(128, dtype=jnp.int32) % 8)[None, None, :]
        channel = serial % 4
        at = jnp.where(channel == 1, at_x, jnp.where(channel == 2, at_y, at_z))
        limit = jnp.where(channel == 1, total_x, jnp.where(channel == 2, total_y, CZ))
        in_grid = (at_x >= 0) & (at_x < total_x) & (at_y >= 0) & (at_y < total_y)
        inside = ((at >= 2) & (at < limit - 2) & (channel > 0) & in_grid).astype(F32)
        return inside

    def places(block, move):
        known = block[:, 0:4, 0:bins].astype(jnp.int32)
        y = known[:, 1] + LOW_Y + move
        row = known[:, 0] * ROWS_X + 4 * y
        good = (known[:, 3] > 0) & (y >= 0) & (y <= LOW_Y + TILE + 1)
        return jnp.where(good, row, -1).reshape(-1), known[:, 2].reshape(-1)

    step_a = jnp.where(place_y % 2 == 0, TILE, -TILE)
    for substep in range(SUBSTEPS):
        column = column_of(payload)
        beside_a, beside_b = neighbour_of(column, 0), neighbour_of(column, 1)
        if substep == 0:
            own = payload[4 * bins : 4 * bins + 3, 0:bins].astype(jnp.int32)
            own_row = own[0] * ROWS_X + 4 * (own[1] + LOW_Y)
            anchor_z = own[2]
            late, _ = lax.optimization_barrier((payload[4 * bins : 4 * bins + 3], column))
            late = late[:, 0:bins].astype(jnp.int32)
            inside = inside_grid(late[0] - 2, late[1], late[2])
            row, z = places(column[:, 4 * bins :], 0)
            column_tabs = jnp.concatenate([own_row, row, anchor_z, z])
        compact = run_column(total_x, bins, column_tabs, column)
        listing = substep == 0
        if listing:
            facts_a, facts_b, _ = lax.optimization_barrier(
                (beside_a[:, 4 * bins :], beside_b[:, 4 * bins :], compact)
            )
            row_a, z_a = places(facts_a, step_a)
            row_b, z_b = places(facts_b, -step_a)
            tabs_a = jnp.concatenate([own_row, row_a, anchor_z, z_a])
            tabs_b = jnp.concatenate([own_row, row_b, anchor_z, z_b])
        last = substep == SUBSTEPS - 1
        results = run_kernel(
            False,
            listing,
            last,
            total_x,
            bins,
            [tabs_a] + ([tabs_b] if listing else [list_a, list_b])
            + [beside_a, beside_b, compact, inside, state, params, depth],
        )
        if not last:
            payload, state, params, depth = results[:4]
        if listing:
            list_a, list_b = results[4:]
    return tuple(turn(array) for array in results)


def solution(mesh):
    wide = P(("runs", "gx", "gy"), None, None)
    flat = P(("runs", "gx", "gy"), None)
    return jax.shard_map(
        shards,
        mesh=mesh,
        in_specs=(wide, flat, wide, wide, wide, flat, flat, flat, P(("runs", "gx", "gy"))),
        out_specs=(wide, wide, wide),
        check_vma=False,
    )
```
